256 devices in a mesh: dp: 32 (over z_lo, x, y), tensor: 8 (over z_hi, core).
Axes of the slice: x: 4, y: 4, z: 8 (z_hi: 4, z_lo: 2; z = z_hi * 2 + z_lo), core: 2. Of those that a mesh axis runs over, the one named last changes fastest.
Arguments:
- hidden: bfloat16 [16384, 4096], P(('dp', 'tensor')), may hold values from -24 to 24
- adapter: bfloat16 [4096, 9216], P(None, 'tensor'), may hold values from -0.09375 to 0.09375
- teacher_rows: bfloat16 [16384, 9216], P('dp', 'tensor')
- scale_exps: int32 [16384], P('dp'), may hold values from -1 to 1
- packing: int32 [16384], P('dp'), may hold values from 0 to 16383, as said below
Outputs:
- row_grad: bfloat16 [16384, 4096], P(('dp', 'tensor'))
- weight_grad: bfloat16 [4096, 9216], P('dp', 'tensor')
The draws below stay inside these ranges and needn't reach their ends.
Inputs may be any that keep to these rules, and one draw needn't show every extreme that they name: packing is a permutation of the tokens; each aligned block of 512 packed rows holds exactly 16 tokens of each block of 512 consecutive tokens.
All inputs are finite; a program needn't handle non-finite values.
Results may differ from the reference program's by a relative error of at most 0.0036.
Values may be sent and summed in bfloat16 or wider, within the bound.
No kernel may reach another device: no remote copies, remote signals or barrier semaphores. Data moves between devices by JAX's collectives and lax.ppermute only.
A program may use at most 128 MiB of HBM per device.

```python
import math
import jax
import jax.numpy as jnp
from jax import lax

D = 4096
TW = 9216
TOK_DEV = 512
TOKENS = 16384
N_DP = 32


def draw_packing(key, part):
    key = jax.random.fold_in(key, 11)
    key_first, key_second = jax.random.split(key)
    share = TOK_DEV // N_DP
    first = jax.vmap(lambda sub: jax.random.permutation(sub, TOK_DEV))(jax.random.split(key_first, N_DP))
    tokens = first.astype(jnp.int32) + (jnp.arange(N_DP, dtype=jnp.int32) * TOK_DEV)[:, None]
    by_teacher = tokens.reshape(N_DP, N_DP, share).transpose(1, 0, 2).reshape(N_DP, TOK_DEV)
    second = jax.vmap(lambda sub: jax.random.permutation(sub, TOK_DEV))(jax.random.split(key_second, N_DP))
    packed = jnp.take_along_axis(by_teacher, second.astype(jnp.int32), axis=1)
    return packed.reshape(TOKENS).astype(jnp.int32)


def draw_teacher_rows(key, part):
    key = jax.random.fold_in(key, 12)
    key_values, key_columns = jax.random.split(key, 2)
    column = jnp.arange(TW, dtype=jnp.float32) / TW
    spread = jnp.exp(jax.random.uniform(key_columns, (TW,), jnp.float32, math.log(0.5), math.log(2.0)))
    values = jax.random.normal(key_values, (TOKENS, TW), jnp.float32)
    ramp = 3.0 ** (column - 0.5)
    return (values * (ramp * spread)[None, :]).astype(jnp.bfloat16)


def place_ends(result, own_key, low, top_value):
    longest = result.shape.index(max(result.shape))
    spots = []
    for shift in (0, 1):
        where = [jax.random.randint(jax.random.fold_in(own_key, axis), (), 0, length) for axis, length in enumerate(result.shape)]
        where[longest] = (where[longest] + shift) % result.shape[longest]
        spots.append(tuple(where))
    return result.at[spots[0]].set(low).at[spots[1]].set(top_value)


def strengthened(entries, stream_key, source, target, parts, factor):
    def block_of(axis_at):
        return (jnp.arange(entries.shape[axis_at]) // (entries.shape[axis_at] // parts)).reshape((-1,) + (1,) * (entries.ndim - 1 - axis_at))

    first = jax.random.permutation(stream_key, parts)[block_of(target)]
    other_side = (block_of(target) + parts // 2) % parts
    return jnp.where((block_of(source) == first) | (block_of(source) == other_side), factor * entries, entries)


def steps_of(rng, shape, cuts, low, top_value):
    gain = 1.0
    for position, blocks in cuts:
        steps = jax.random.uniform(jax.random.fold_in(jax.random.fold_in(rng, 6), position), (blocks,), jnp.float32, low / len(cuts), top_value / len(cuts))
        gain = gain * jnp.repeat(jnp.exp(steps), shape[position] // blocks).reshape((-1,) + (1,) * (len(shape) - 1 - position))
    return gain


def noise(key, shape, deviation, most, cuts=(), held_as=jnp.bfloat16):
    factor_of = steps_of(key, shape, cuts, -0.22, 0.18) if cuts else 1.0
    entries = jax.random.normal(key, shape, jnp.float32) * deviation * factor_of
    return jnp.minimum(jnp.maximum(entries, -most), most).astype(held_as)


def gaussian_with(rng, dims, scale, reach, cuts, heavy, held_as=jnp.bfloat16):
    result = scale * jax.random.normal(rng, dims, jnp.float32)
    if cuts:
        result = result * steps_of(rng, dims, cuts, -0.22, 0.18)
    return jnp.clip(strengthened(result, jax.random.fold_in(rng, 3), *heavy), -reach, reach).astype(held_as)


def setup_inputs(seed: int = 0) -> dict:
    splits = jax.random.split(jax.random.key(seed), 6)
    return {
        "hidden": gaussian_with(splits[0], (TOKENS, D), 1.0, 24.0, ((0, 256),), (0, 1, 256, 6.0)),
        "adapter": noise(splits[1], (D, TW), D ** -0.5, 0.09375, ((1, 8),)),
        "teacher_rows": draw_teacher_rows(jax.random.fold_in(splits[5], 71), 0),
        "scale_exps": place_ends(jax.random.randint(splits[3], (TOKENS,), -1, 2), jax.random.fold_in(splits[3], 1), -1, 1).astype(jnp.int32),
        "packing": draw_packing(jax.random.fold_in(splits[5], 71), 0),
    }


def reference(hidden, adapter, teacher_rows, scale_exps, packing):
    order = jnp.argsort(packing).astype(jnp.int32)

    def shard(carry, index):
        start = (index * TOK_DEV).astype(jnp.int32)
        rows_h = lax.dynamic_slice_in_dim(hidden, start, TOK_DEV, 0)
        picks = lax.dynamic_slice_in_dim(order, start, TOK_DEV, 0)
        scales = jnp.exp2(scale_exps[picks].astype(jnp.float32))
        target = teacher_rows[picks].astype(jnp.float32) * scales[:, None]
        projected = jnp.dot(rows_h, adapter, preferred_element_type=jnp.float32)
        energy = jnp.sum(target * target, axis=1) / TW + 1e-5
        delta = ((projected - target) / energy[:, None]).astype(jnp.bfloat16)
        row_total = jnp.dot(delta, adapter.T, preferred_element_type=jnp.float32)
        partial_w = jnp.dot(rows_h.T, delta, preferred_element_type=jnp.float32)
        carry = carry + partial_w
        return carry, row_total.astype(jnp.bfloat16)

    total, grads = lax.scan(shard, jnp.zeros((D, TW), jnp.float32), jnp.arange(N_DP, dtype=jnp.int32))
    return grads.reshape(TOKENS, D), (total / TOK_DEV).astype(jnp.bfloat16)
```

```python
import functools

import jax
import jax.numpy as jnp
from jax import lax
from jax.experimental import pallas as pl
from jax.experimental.pallas import tpu as pltpu
from jax.sharding import PartitionSpec as P

TW = 9216
META = 128
F32, BF16 = jnp.float32, jnp.bfloat16


def params(mib):
    return pltpu.CompilerParams(vmem_limit_bytes=mib << 20)


LIGHT = pl.CostEstimate(flops=0, bytes_accessed=0, transcendentals=0)


def iota(shape, axis):
    return lax.broadcasted_iota(jnp.int32, shape, axis)


def column(row):
    return jnp.broadcast_to(row.astype(F32), (META, row.shape[1])).T


def as_row(col):
    return jnp.broadcast_to(col, (col.shape[0], META)).T[:1]


def scale_of(exps):
    return jnp.where(exps > 0.5, 2.0, jnp.where(exps < -0.5, 0.5, 1.0))


def squares_kernel(exps_ref, rows_ref, squares_ref):
    rows = rows_ref[...].astype(F32)
    scale = scale_of(exps_ref[...].astype(F32))
    squares_ref[...] = as_row(jnp.sum(rows * rows, axis=1, keepdims=True)) * (scale * scale)


def sum_kernel(*refs):
    total = refs[0][...]
    for ref in refs[1:-1]:
        total = total + ref[...]
    refs[-1][...] = total


def pack_kernel(share, where_ref, packing_ref, exps_ref, s0_ref, s1_ref, s2_ref, s3_ref, rows_ref, keep_ref, leave_ref):
    tok, width = rows_ref.shape
    packing = packing_ref[...]
    peer = packing // tok
    slot = packing % tok
    plane = tok // share // 2
    peer = jnp.where(peer // plane == where_ref[0], 0, plane) + peer % plane
    earlier = iota((tok, tok), 0) < iota((tok, tok), 1)
    same = (column(peer)[:, :1] == peer.astype(F32)) & earlier
    rank = jnp.sum(jnp.where(same, 1.0, 0.0), axis=0, keepdims=True)
    place = peer * share + rank.astype(jnp.int32)
    pick = jnp.where(iota((tok, tok), 0) == place, 1.0, 0.0).astype(BF16)
    lane = iota((tok, META), 1)
    meta = jnp.where(lane == 0, column(slot // 16), 0.0)
    meta = jnp.where(lane == 1, column(slot % 16), meta)
    meta = jnp.where(lane == 2, column(exps_ref[...]), meta)
    rest = column(s0_ref[...] + s1_ref[...] + s2_ref[...] + s3_ref[...])
    for k in range(3):
        term = rest.astype(BF16).astype(F32)
        meta = jnp.where(lane == 3 + k, term, meta)
        rest = rest - term
    rows = jnp.dot(pick, rows_ref[...], preferred_element_type=F32).astype(BF16)
    meta = jnp.dot(pick, meta.astype(BF16), preferred_element_type=F32).astype(BF16)
    half = tok // 2
    for out_ref, at in ((keep_ref, 0), (leave_ref, half)):
        out_ref[:, :width] = rows[at : at + half]
        out_ref[:, width:] = meta[at : at + half]


def merge_kernel(share, keep_ref, came_ref, out_ref):
    for side, rows_ref in enumerate((keep_ref, came_ref)):
        for peer in range(rows_ref.shape[0] // share):
            out_ref[peer, side * share : (side + 1) * share, :] = rows_ref[peer * share : (peer + 1) * share, :]


def place_kernel(got_ref, target_ref, energy_ref):
    tok, width = target_ref.shape
    meta = got_ref[:, width:].astype(F32).T
    slot = (meta[0:1] * 16.0 + meta[1:2]).astype(jnp.int32)
    here = iota((tok, tok), 0) == slot
    pick = jnp.where(here, 1.0, 0.0).astype(BF16)

    def placed(row):
        return jnp.sum(jnp.where(here, row, 0.0), axis=1, keepdims=True)

    rows = jnp.dot(pick, got_ref[:, :width], preferred_element_type=F32)
    target_ref[...] = (rows * placed(scale_of(meta[2:3]))).astype(BF16)
    squares = placed(meta[3:4] + meta[4:5] + meta[5:6])
    energy_ref[...] = jnp.broadcast_to(squares / TW + 1e-05, (tok, META))


def project_kernel(own_ref, sib_ref, adapter_ref, out_ref):
    rows = jnp.concatenate([own_ref[...], sib_ref[...]], axis=0)
    out_ref[...] = jnp.dot(rows, adapter_ref[...], preferred_element_type=F32)


def project_call(own, sib, adapter):
    half, depth = own.shape
    width = adapter.shape[1]
    tile = 384
    return pl.pallas_call(
        project_kernel,
        out_shape=jax.ShapeDtypeStruct((2 * half, width), F32),
        grid=(width // tile,),
        in_specs=[
            pl.BlockSpec((half, depth), lambda n: (0, 0)),
            pl.BlockSpec((half, depth), lambda n: (0, 0)),
            pl.BlockSpec((depth, tile), lambda n: (0, n)),
        ],
        out_specs=pl.BlockSpec((2 * half, tile), lambda n: (0, n)),
        compiler_params=params(14),
        cost_estimate=LIGHT,
        name="project",
    )(own, sib, adapter)


def delta_kernel(where_ref, p0_ref, p1_ref, p2_ref, p3_ref, target_ref, energy_ref, delta_ref):
    half = p0_ref.shape[0] // 2
    zh, core = where_ref[3], where_ref[4]
    step = 1 - 2 * core
    for s, p_ref in enumerate((p0_ref, p1_ref, p2_ref, p3_ref)):
        mine = ((zh - step * s + 4) % 4) * 2 + core
        sibs = ((zh + step * s + 4) % 4) * 2 + 1 - core
        for side, block in enumerate((mine, sibs)):
            token = pl.ds(pl.multiple_of(block * half, half), half)
            diff = p_ref[side * half : (side + 1) * half, :] - target_ref[token, :].astype(F32)
            at = (2 * s + side) * half
            delta_ref[at : at + half, :] = (diff / energy_ref[token, :1]).astype(BF16)


def row_kernel(delta_ref, adapter_ref, *refs):
    keeps, send_ref = refs[:4], refs[4]
    half = keeps[0].shape[0]
    term = lax.dot_general(delta_ref[...], adapter_ref[...], (((1,), (1,)), ((), ())), preferred_element_type=F32)
    for s in range(4):
        keeps[s][...] = term[2 * s * half : (2 * s + 1) * half]
        send_ref[s * half : (s + 1) * half, :] = term[(2 * s + 1) * half : (2 * s + 2) * half].astype(BF16)


def row_call(delta, adapter):
    tok, width = delta.shape
    half = tok // 8
    depth = adapter.shape[0]
    tile = 512
    return pl.pallas_call(
        row_kernel,
        out_shape=(jax.ShapeDtypeStruct((half, depth), F32),) * 4 + (jax.ShapeDtypeStruct((4 * half, depth), BF16),),
        grid=(depth // tile,),
        in_specs=[
            pl.BlockSpec((tok, width), lambda n: (0, 0)),
            pl.BlockSpec((tile, width), lambda n: (n, 0)),
        ],
        out_specs=(pl.BlockSpec((half, tile), lambda n: (0, n)),) * 4
        + (pl.BlockSpec((4 * half, tile), lambda n: (0, n)),),
        compiler_params=params(11),
        cost_estimate=LIGHT,
        name="row_terms",
    )(delta, adapter)


def weight_kernel(k, with_came, turn, where_ref, *refs):
    hidden, delta = refs[:8], refs[8]
    came = refs[9:11] if with_came else (None, None)
    outs, left = refs[9 + 2 * with_came : -1], refs[-1]
    half = hidden[0].shape[0]
    x, y, core = where_ref[1], where_ref[2], where_ref[4]
    ahead = k * (1 - 2 * core) + 4
    for chunk in range(2):
        for j in range(4):
            if chunk == 0:
                block = ((x + ahead) % 4) * 4 + (y + j) % 4
            else:
                block = 16 + ((x + j) % 4) * 4 + (y + ahead) % 4
            columns = pl.ds(pl.multiple_of(block * 128, 128), 128)
            for part in range(8):
                left[part * half : (part + 1) * half, j * 128 : (j + 1) * 128] = hidden[part][:, columns]
        term = lax.dot_general(left[...], delta[...], (((0,), (0,)), ((), ())), preferred_element_type=F32)
        if with_came:
            term = term + came[chunk][...].astype(F32)
        if turn:
            for j in range(4):
                out = outs[4 * chunk + j]
                out[...] = term[128 * j : 128 * (j + 1)].astype(out.dtype)
        else:
            outs[chunk][...] = term.astype(BF16)


def weight_call(k, where, hidden, delta, came=()):
    tokens = 8 * hidden[0].shape[0]
    width = delta.shape[1]
    vmem = pl.BlockSpec(memory_space=pltpu.VMEM)
    turn = k == 0
    if turn:
        kinds = [jax.ShapeDtypeStruct((128, width), F32)] + [jax.ShapeDtypeStruct((128, width), BF16)] * 3
    else:
        kinds = [jax.ShapeDtypeStruct((512, width), BF16)]
    return pl.pallas_call(
        functools.partial(weight_kernel, k, len(came) > 0, turn),
        out_shape=tuple(kinds * 2),
        in_specs=[pl.BlockSpec(memory_space=pltpu.SMEM)] + [vmem] * (9 + len(came)),
        out_specs=(vmem,) * (2 * len(kinds)),
        scratch_shapes=[pltpu.VMEM((tokens, 512), BF16)],
        compiler_params=params(18),
        cost_estimate=LIGHT,
        name=f"weight_{k}",
    )(where, *hidden, delta, *came)


def light(kernel, name, out_shape, mib, *args, scalars=0):
    vmem = pl.BlockSpec(memory_space=pltpu.VMEM)
    return pl.pallas_call(
        kernel,
        out_shape=tuple(out_shape),
        in_specs=[pl.BlockSpec(memory_space=pltpu.SMEM)] * scalars + [vmem] * (len(args) - scalars),
        out_specs=(vmem,) * len(out_shape),
        compiler_params=params(mib),
        cost_estimate=LIGHT,
        name=name,
    )(*args)


def shard_kernel(where, own_a, a1, a2, a3, own_b, b1, b2, b3, stay, leave):
    sum_a = own_a[...] + a1[...].astype(F32) + a2[...].astype(F32) + a3[...].astype(F32)
    sum_b = own_b[...] + b1[...].astype(F32) + b2[...].astype(F32) + b3[...].astype(F32)
    low = where[0] == 0
    stay[...] = jnp.where(low, sum_a, sum_b)
    leave[...] = jnp.where(low, sum_b, sum_a).astype(BF16)


def weight_out_kernel(tokens, stay, came, out):
    out[...] = ((stay[...] + came[...].astype(F32)) / tokens).astype(BF16)


def row_out_kernel(pair, came, out):
    out[...] = (pair[...] + came[...].astype(F32)).astype(BF16)


def pair_kernel(k0, k1, k2, k3, swapped, *outs):
    half = k0.shape[0]
    for s, keep in enumerate((k0, k1, k2, k3)):
        total = keep[...] + swapped[s * half : (s + 1) * half, :].astype(F32)
        outs[s][...] = total.astype(outs[s].dtype)


def on_device(hidden, adapter, teacher_rows, scale_exps, packing):
    tok, width = teacher_rows.shape
    half = hidden.shape[0]
    peers = lax.axis_size("dp")
    dp, tensor = lax.axis_index("dp"), lax.axis_index("tensor")
    zl, x, y = dp // 16, (dp // 4) % 4, dp % 4
    zh, core = tensor // 2, tensor % 2

    def over_dp(move):
        pairs = []
        for i in range(32):
            a, b, c = move(i // 16, (i // 4) % 4, i % 4)
            pairs.append((i, (a % 2) * 16 + (b % 4) * 4 + c % 4))
        return lambda value: lax.ppermute(value, "dp", pairs)

    def over_tensor(move):
        pairs = []
        for i in range(8):
            a, b = move(i // 2, i % 2)
            pairs.append((i, (a % 4) * 2 + b % 2))
        return lambda value: lax.ppermute(value, "tensor", pairs)

    def by_core(move):
        pairs = []
        for i in range(256):
            d, t = i // 8, i % 8
            b, c = move((d // 4) % 4, d % 4, 1 - 2 * (t % 2))
            pairs.append((i, ((d // 16) * 16 + (b % 4) * 4 + c % 4) * 8 + t))
        return lambda value: lax.ppermute(value, ("dp", "tensor"), pairs)

    x_ring = by_core(lambda b, c, way: (b + way, c))
    y_ring = by_core(lambda b, c, way: (b, c + way))
    x_forth, x_back = over_dp(lambda a, b, c: (a, b + 1, c)), over_dp(lambda a, b, c: (a, b - 1, c))
    y_forth, y_back = over_dp(lambda a, b, c: (a, b, c + 1)), over_dp(lambda a, b, c: (a, b, c - 1))
    x_across, y_across = over_dp(lambda a, b, c: (a, b + 2, c)), over_dp(lambda a, b, c: (a, b, c + 2))
    z_swap = over_dp(lambda a, b, c: (a + 1, b, c))
    core_swap = over_tensor(lambda a, b: (a, b + 1))
    chain = over_tensor(lambda a, b: (a + 1 - 2 * b, b))

    where = jnp.stack([zl, x, y, zh, core]).astype(jnp.int32)
    row = jax.ShapeDtypeStruct((1, tok), F32)
    share = tok // peers
    lanes = width + META
    packing, scale_exps = packing.reshape(1, tok), scale_exps.reshape(1, tok)

    own = [hidden, chain(hidden)]
    squares = light(squares_kernel, "squares", (row,), 10, scale_exps, teacher_rows)[0]
    squares = light(sum_kernel, "pair_squares", (row,), 4, squares, core_swap(squares))[0]
    others = [over_tensor(lambda a, b, k=k: (a + k, b))(squares) for k in (1, 2, 3)]
    half_rows = jax.ShapeDtypeStruct((tok // 2, lanes), BF16)
    keep, leave = light(
        functools.partial(pack_kernel, share), "pack", (half_rows, half_rows), 18,
        where, packing, scale_exps, squares, *others, teacher_rows, scalars=1,
    )
    own[1], keep = lax.optimization_barrier((own[1], keep))
    came = z_swap(leave)
    own.append(chain(own[1]))
    sib = [core_swap(block) for block in own]
    projected = [project_call(own[s], sib[s], adapter) for s in range(2)]
    came, *projected = lax.optimization_barrier((came, *projected))
    own.append(chain(own[2]))
    sib.append(core_swap(own[3]))
    projected += [project_call(own[s], sib[s], adapter) for s in range(2, 4)]
    merged = light(
        functools.partial(merge_kernel, share), "merge",
        (jax.ShapeDtypeStruct((peers // 2, 2 * share, lanes), BF16),), 10, keep, came,
    )[0]
    groups = [list(range(peers // 2)), list(range(peers // 2, peers))]
    got = lax.all_to_all(merged, "dp", 0, 0, axis_index_groups=groups, tiled=True)
    got, *projected[2:] = lax.optimization_barrier((got, *projected[2:]))
    target, energy = light(
        place_kernel, "place",
        (jax.ShapeDtypeStruct((tok, width), BF16), jax.ShapeDtypeStruct((tok, META), F32)), 16,
        got.reshape(tok, lanes),
    )
    delta = light(
        delta_kernel, "delta", (jax.ShapeDtypeStruct((tok, width), BF16),), 12,
        where, *projected, target, energy, scalars=1,
    )[0]

    held = [part for pair in zip(own, sib) for part in pair]
    ring_a, ring_b = weight_call(3, where, held, delta)
    came = (x_ring(ring_a), y_ring(ring_b))
    later, _ = lax.optimization_barrier((delta, ring_a))
    *keeps, send = row_call(later, adapter)
    *came, send = lax.optimization_barrier((*came, send))
    swapped = core_swap(send)
    ring_a, ring_b = weight_call(2, where, held, delta, came)
    came = (x_ring(ring_a), y_ring(ring_b))
    block = jax.ShapeDtypeStruct((half, hidden.shape[1]), F32)
    block16 = jax.ShapeDtypeStruct(block.shape, BF16)
    swapped, _ = lax.optimization_barrier((swapped, ring_a))
    pair = light(pair_kernel, "pair", (block, block16, block, block), 14, *keeps, swapped)
    total = chain(pair[1])
    *came, total = lax.optimization_barrier((*came, total))
    ring_a, ring_b = weight_call(1, where, held, delta, came)
    came = (x_ring(ring_a), y_ring(ring_b))
    total, _ = lax.optimization_barrier((total, ring_a))
    total = chain(light(row_out_kernel, "row_2", (block16,), 8, pair[2], total)[0])
    *came, total = lax.optimization_barrier((*came, total))
    own_a, a1, a2, a3, own_b, b1, b2, b3 = weight_call(0, where, held, delta, came)
    total, _ = lax.optimization_barrier((total, a1))
    total = chain(light(row_out_kernel, "row_3", (block16,), 8, pair[3], total)[0])
    came = (y_forth(a1), y_across(a2), y_back(a3), x_forth(b1), x_across(b2), x_back(b3))
    *came, total = lax.optimization_barrier((*came, total))
    part = jax.ShapeDtypeStruct((128, width), F32)
    part16 = jax.ShapeDtypeStruct((128, width), BF16)
    stay, leave = light(
        shard_kernel, "shard", (part, part16), 10, where, own_a, *came[:3], own_b, *came[3:], scalars=1,
    )
    weight_grad = light(
        functools.partial(weight_out_kernel, tok), "weight_out", (part16,), 8, stay, z_swap(leave)
    )[0]
    row_grad = light(row_out_kernel, "row_0", (block16,), 8, pair[0], total)[0]
    return row_grad, weight_grad


def solution(mesh):
    placed = (P(("dp", "tensor"), None), P(None, "tensor"), P("dp", "tensor"), P("dp"), P("dp"))
    return jax.shard_map(
        on_device,
        mesh=mesh,
        in_specs=placed,
        out_specs=(P(("dp", "tensor"), None), P("dp", "tensor")),
        check_vma=False,
    )
```

```python
import functools

import jax
import jax.numpy as jnp
from jax import lax
from jax.experimental import pallas as pl
from jax.experimental.pallas import tpu as pltpu
from jax.sharding import PartitionSpec as P

TW = 9216
META = 128
F32, BF16 = jnp.float32, jnp.bfloat16


def params(mib):
    return pltpu.CompilerParams(vmem_limit_bytes=mib << 20)


LIGHT = pl.CostEstimate(flops=0, bytes_accessed=0, transcendentals=0)


def iota(shape, axis):
    return lax.broadcasted_iota(jnp.int32, shape, axis)


def column(row):
    return jnp.broadcast_to(row.astype(F32), (META, row.shape[1])).T


def as_row(col):
    return jnp.broadcast_to(col, (col.shape[0], META)).T[:1]


def scale_of(exps):
    return jnp.where(exps > 0.5, 2.0, jnp.where(exps < -0.5, 0.5, 1.0))


def squares_kernel(exps_ref, rows_ref, squares_ref):
    rows = rows_ref[...].astype(F32)
    scale = scale_of(exps_ref[...].astype(F32))
    squares_ref[...] = as_row(jnp.sum(rows * rows, axis=1, keepdims=True)) * (scale * scale)


def sum_kernel(*refs):
    total = refs[0][...]
    for ref in refs[1:-1]:
        total = total + ref[...]
    refs[-1][...] = total


def pack_kernel(share, where_ref, packing_ref, exps_ref, s0_ref, s1_ref, s2_ref, s3_ref, rows_ref, keep_ref, leave_ref):
    tok, width = rows_ref.shape
    packing = packing_ref[...]
    peer = packing // tok
    slot = packing % tok
    plane = tok // share // 2
    peer = jnp.where(peer // plane == where_ref[0], 0, plane) + peer % plane
    earlier = iota((tok, tok), 0) < iota((tok, tok), 1)
    same = (column(peer)[:, :1] == peer.astype(F32)) & earlier
    rank = jnp.sum(jnp.where(same, 1.0, 0.0), axis=0, keepdims=True)
    place = peer * share + rank.astype(jnp.int32)
    pick = jnp.where(iota((tok, tok), 0) == place, 1.0, 0.0).astype(BF16)
    lane = iota((tok, META), 1)
    meta = jnp.where(lane == 0, column(slot // 16), 0.0)
    meta = jnp.where(lane == 1, column(slot % 16), meta)
    meta = jnp.where(lane == 2, column(exps_ref[...]), meta)
    rest = column(s0_ref[...] + s1_ref[...] + s2_ref[...] + s3_ref[...])
    for k in range(3):
        term = rest.astype(BF16).astype(F32)
        meta = jnp.where(lane == 3 + k, term, meta)
        rest = rest - term
    rows = jnp.dot(pick, rows_ref[...], preferred_element_type=F32).astype(BF16)
    meta = jnp.dot(pick, meta.astype(BF16), preferred_element_type=F32).astype(BF16)
    half = tok // 2
    for out_ref, at in ((keep_ref, 0), (leave_ref, half)):
        out_ref[:, :width] = rows[at : at + half]
        out_ref[:, width:] = meta[at : at + half]


def merge_kernel(share, keep_ref, came_ref, out_ref):
    for side, rows_ref in enumerate((keep_ref, came_ref)):
        for peer in range(rows_ref.shape[0] // share):
            out_ref[peer, side * share : (side + 1) * share, :] = rows_ref[peer * share : (peer + 1) * share, :]


def place_kernel(got_ref, target_ref, energy_ref):
    tok, width = target_ref.shape
    meta = got_ref[:, width:].astype(F32).T
    slot = (meta[0:1] * 16.0 + meta[1:2]).astype(jnp.int32)
    here = iota((tok, tok), 0) == slot
    pick = jnp.where(here, 1.0, 0.0).astype(BF16)

    def placed(row):
        return jnp.sum(jnp.where(here, row, 0.0), axis=1, keepdims=True)

    rows = jnp.dot(pick, got_ref[:, :width], preferred_element_type=F32)
    target_ref[...] = (rows * placed(scale_of(meta[2:3]))).astype(BF16)
    squares = placed(meta[3:4] + meta[4:5] + meta[5:6])
    energy_ref[...] = jnp.broadcast_to(squares / TW + 1e-05, (tok, META))


def project_kernel(own_ref, sib_ref, adapter_ref, out_ref):
    rows = jnp.concatenate([own_ref[...], sib_ref[...]], axis=0)
    out_ref[...] = jnp.dot(rows, adapter_ref[...], preferred_element_type=F32)


def project_call(own, sib, adapter):
    half, depth = own.shape
    width = adapter.shape[1]
    tile = 384
    return pl.pallas_call(
        project_kernel,
        out_shape=jax.ShapeDtypeStruct((2 * half, width), F32),
        grid=(width // tile,),
        in_specs=[
            pl.BlockSpec((half, depth), lambda n: (0, 0)),
            pl.BlockSpec((half, depth), lambda n: (0, 0)),
            pl.BlockSpec((depth, tile), lambda n: (0, n)),
        ],
        out_specs=pl.BlockSpec((2 * half, tile), lambda n: (0, n)),
        compiler_params=params(14),
        cost_estimate=LIGHT,
        name="project",
    )(own, sib, adapter)


def delta_kernel(where_ref, p0_ref, p1_ref, p2_ref, p3_ref, target_ref, energy_ref, delta_ref):
    half = p0_ref.shape[0] // 2
    zh, core = where_ref[3], where_ref[4]
    step = 1 - 2 * core
    for s, p_ref in enumerate((p0_ref, p1_ref, p2_ref, p3_ref)):
        mine = ((zh - step * s + 4) % 4) * 2 + core
        sibs = ((zh + step * s + 4) % 4) * 2 + 1 - core
        for side, block in enumerate((mine, sibs)):
            token = pl.ds(pl.multiple_of(block * half, half), half)
            diff = p_ref[side * half : (side + 1) * half, :] - target_ref[token, :].astype(F32)
            at = (2 * s + side) * half
            delta_ref[at : at + half, :] = (diff / energy_ref[token, :1]).astype(BF16)


def row_kernel(delta_ref, adapter_ref, *refs):
    keeps, send_ref = refs[:4], refs[4]
    half = keeps[0].shape[0]
    term = lax.dot_general(delta_ref[...], adapter_ref[...], (((1,), (1,)), ((), ())), preferred_element_type=F32)
    for s in range(4):
        keeps[s][...] = term[2 * s * half : (2 * s + 1) * half]
        send_ref[s * half : (s + 1) * half, :] = term[(2 * s + 1) * half : (2 * s + 2) * half].astype(BF16)


def row_call(delta, adapter):
    tok, width = delta.shape
    half = tok // 8
    depth = adapter.shape[0]
    tile = 512
    return pl.pallas_call(
        row_kernel,
        out_shape=(jax.ShapeDtypeStruct((half, depth), F32),) * 4 + (jax.ShapeDtypeStruct((4 * half, depth), BF16),),
        grid=(depth // tile,),
        in_specs=[
            pl.BlockSpec((tok, width), lambda n: (0, 0)),
            pl.BlockSpec((tile, width), lambda n: (n, 0)),
        ],
        out_specs=(pl.BlockSpec((half, tile), lambda n: (0, n)),) * 4
        + (pl.BlockSpec((4 * half, tile), lambda n: (0, n)),),
        compiler_params=params(11),
        cost_estimate=LIGHT,
        name="row_terms",
    )(delta, adapter)


def weight_kernel(k, with_came, turn, where_ref, *refs):
    hidden, delta = refs[:8], refs[8]
    came = refs[9:11] if with_came else (None, None)
    outs, left = refs[9 + 2 * with_came : -1], refs[-1]
    half = hidden[0].shape[0]
    x, y, core = where_ref[1], where_ref[2], where_ref[4]
    ahead = k * (1 - 2 * core) + 4
    for chunk in range(2):
        for j in range(4):
            if chunk == 0:
                block = ((x + ahead) % 4) * 4 + (y + j) % 4
            else:
                block = 16 + ((x + j) % 4) * 4 + (y + ahead) % 4
            columns = pl.ds(pl.multiple_of(block * 128, 128), 128)
            for part in range(8):
                left[part * half : (part + 1) * half, j * 128 : (j + 1) * 128] = hidden[part][:, columns]
        term = lax.dot_general(left[...], delta[...], (((0,), (0,)), ((), ())), preferred_element_type=F32)
        if with_came:
            term = term + came[chunk][...].astype(F32)
        if turn:
            for j in range(4):
                out = outs[4 * chunk + j]
                out[...] = term[128 * j : 128 * (j + 1)].astype(out.dtype)
        else:
            outs[chunk][...] = term.astype(BF16)


def weight_call(k, where, hidden, delta, came=()):
    tokens = 8 * hidden[0].shape[0]
    width = delta.shape[1]
    vmem = pl.BlockSpec(memory_space=pltpu.VMEM)
    turn = k == 0
    if turn:
        kinds = [jax.ShapeDtypeStruct((128, width), F32)] + [jax.ShapeDtypeStruct((128, width), BF16)] * 3
    else:
        kinds = [jax.ShapeDtypeStruct((512, width), BF16)]
    return pl.pallas_call(
        functools.partial(weight_kernel, k, len(came) > 0, turn),
        out_shape=tuple(kinds * 2),
        in_specs=[pl.BlockSpec(memory_space=pltpu.SMEM)] + [vmem] * (9 + len(came)),
        out_specs=(vmem,) * (2 * len(kinds)),
        scratch_shapes=[pltpu.VMEM((tokens, 512), BF16)],
        compiler_params=params(18),
        cost_estimate=LIGHT,
        name=f"weight_{k}",
    )(where, *hidden, delta, *came)


def light(kernel, name, out_shape, mib, *args, scalars=0):
    vmem = pl.BlockSpec(memory_space=pltpu.VMEM)
    return pl.pallas_call(
        kernel,
        out_shape=tuple(out_shape),
        in_specs=[pl.BlockSpec(memory_space=pltpu.SMEM)] * scalars + [vmem] * (len(args) - scalars),
        out_specs=(vmem,) * len(out_shape),
        compiler_params=params(mib),
        cost_estimate=LIGHT,
        name=name,
    )(*args)


def shard_kernel(where, own_a, a1, a2, a3, own_b, b1, b2, b3, stay, leave):
    sum_a = own_a[...] + a1[...].astype(F32) + a2[...].astype(F32) + a3[...].astype(F32)
    sum_b = own_b[...] + b1[...].astype(F32) + b2[...].astype(F32) + b3[...].astype(F32)
    low = where[0] == 0
    stay[...] = jnp.where(low, sum_a, sum_b)
    leave[...] = jnp.where(low, sum_b, sum_a).astype(BF16)


def weight_out_kernel(tokens, stay, came, out):
    out[...] = ((stay[...] + came[...].astype(F32)) / tokens).astype(BF16)


def pair_kernel(where, k0, k1, k2, k3, swapped, own, stay, far, near):
    half = k0.shape[0]
    term = [keep[...] + swapped[s * half : (s + 1) * half, :].astype(F32) for s, keep in enumerate((k0, k1, k2, k3))]
    even = where[3] % 2 == 0
    own[...] = term[0]
    stay[...] = jnp.where(even, term[1], term[3])
    far[...] = term[2].astype(BF16)
    near[...] = jnp.where(even, term[3], term[1]).astype(BF16)


def row_mid_kernel(stay, came, send):
    send[...] = (stay[...] + came[...].astype(F32)).astype(BF16)


def row_out_kernel(own, near, end, out):
    out[...] = (own[...] + near[...].astype(F32) + end[...].astype(F32)).astype(BF16)


def on_device(hidden, adapter, teacher_rows, scale_exps, packing):
    tok, width = teacher_rows.shape
    half = hidden.shape[0]
    peers = lax.axis_size("dp")
    dp, tensor = lax.axis_index("dp"), lax.axis_index("tensor")
    zl, x, y = dp // 16, (dp // 4) % 4, dp % 4
    zh, core = tensor // 2, tensor % 2

    def over_dp(move):
        pairs = []
        for i in range(32):
            a, b, c = move(i // 16, (i // 4) % 4, i % 4)
            pairs.append((i, (a % 2) * 16 + (b % 4) * 4 + c % 4))
        return lambda value: lax.ppermute(value, "dp", pairs)

    def over_tensor(move):
        pairs = []
        for i in range(8):
            a, b = move(i // 2, i % 2)
            pairs.append((i, (a % 4) * 2 + b % 2))
        return lambda value: lax.ppermute(value, "tensor", pairs)

    def by_core(move):
        pairs = []
        for i in range(256):
            d, t = i // 8, i % 8
            b, c = move((d // 4) % 4, d % 4, 1 - 2 * (t % 2))
            pairs.append((i, ((d // 16) * 16 + (b % 4) * 4 + c % 4) * 8 + t))
        return lambda value: lax.ppermute(value, ("dp", "tensor"), pairs)

    x_ring = by_core(lambda b, c, way: (b + way, c))
    y_ring = by_core(lambda b, c, way: (b, c + way))
    x_forth, x_back = over_dp(lambda a, b, c: (a, b + 1, c)), over_dp(lambda a, b, c: (a, b - 1, c))
    y_forth, y_back = over_dp(lambda a, b, c: (a, b, c + 1)), over_dp(lambda a, b, c: (a, b, c - 1))
    x_across, y_across = over_dp(lambda a, b, c: (a, b + 2, c)), over_dp(lambda a, b, c: (a, b, c + 2))
    z_swap = over_dp(lambda a, b, c: (a + 1, b, c))
    core_swap = over_tensor(lambda a, b: (a, b + 1))
    row_near = over_tensor(lambda a, b: (a ^ 1 if b == 0 else 3 - a, b))
    row_far = over_tensor(lambda a, b: (3 - a if b == 0 else a ^ 1, b))
    chain = over_tensor(lambda a, b: (a + 1 - 2 * b, b))

    where = jnp.stack([zl, x, y, zh, core]).astype(jnp.int32)
    row = jax.ShapeDtypeStruct((1, tok), F32)
    share = tok // peers
    lanes = width + META
    packing, scale_exps = packing.reshape(1, tok), scale_exps.reshape(1, tok)

    squares = light(squares_kernel, "squares", (row,), 10, scale_exps, teacher_rows)[0]
    squares = light(sum_kernel, "pair_squares", (row,), 4, squares, core_swap(squares))[0]
    others = [over_tensor(lambda a, b, k=k: (a + k, b))(squares) for k in (1, 2, 3)]
    own = [hidden, chain(hidden)]
    own[1], *others = lax.optimization_barrier((own[1], *others))
    half_rows = jax.ShapeDtypeStruct((tok // 2, lanes), BF16)
    keep, leave = light(
        functools.partial(pack_kernel, share), "pack", (half_rows, half_rows), 18,
        where, packing, scale_exps, squares, *others, teacher_rows, scalars=1,
    )
    came = z_swap(leave)
    own.append(chain(own[1]))
    sib = [core_swap(block) for block in own]
    projected = [project_call(own[s], sib[s], adapter) for s in range(3)]
    came, *projected[:2] = lax.optimization_barrier((came, *projected[:2]))
    own.append(chain(own[2]))
    own[3], projected[2] = lax.optimization_barrier((own[3], projected[2]))
    sib.append(core_swap(own[3]))
    projected.append(project_call(own[3], sib[3], adapter))
    merged = light(
        functools.partial(merge_kernel, share), "merge",
        (jax.ShapeDtypeStruct((peers // 2, 2 * share, lanes), BF16),), 10, keep, came,
    )[0]
    groups = [list(range(peers // 2)), list(range(peers // 2, peers))]
    got = lax.all_to_all(merged, "dp", 0, 0, axis_index_groups=groups, tiled=True)
    got, *projected[2:] = lax.optimization_barrier((got, *projected[2:]))
    target, energy = light(
        place_kernel, "place",
        (jax.ShapeDtypeStruct((tok, width), BF16), jax.ShapeDtypeStruct((tok, META), F32)), 16,
        got.reshape(tok, lanes),
    )
    delta = light(
        delta_kernel, "delta", (jax.ShapeDtypeStruct((tok, width), BF16),), 12,
        where, *projected, target, energy, scalars=1,
    )[0]

    held = [part for pair in zip(own, sib) for part in pair]
    ring_a, ring_b = weight_call(3, where, held, delta)
    came = (x_ring(ring_a), y_ring(ring_b))
    later, _ = lax.optimization_barrier((delta, ring_a))
    *keeps, send = row_call(later, adapter)
    *came, send = lax.optimization_barrier((*came, send))
    swapped = core_swap(send)
    ring_a, ring_b = weight_call(2, where, held, delta, came)
    came = (x_ring(ring_a), y_ring(ring_b))
    block = jax.ShapeDtypeStruct((half, hidden.shape[1]), F32)
    block16 = jax.ShapeDtypeStruct(block.shape, BF16)
    swapped, _ = lax.optimization_barrier((swapped, ring_a))
    own_rows, stay, far, near = light(
        pair_kernel, "pair", (block, block, block16, block16), 18, where, *keeps, swapped, scalars=1
    )
    mid = row_near(far)
    *came, mid = lax.optimization_barrier((*came, mid))
    ring_a, ring_b = weight_call(1, where, held, delta, came)
    came = (x_ring(ring_a), y_ring(ring_b))
    mid, near, _ = lax.optimization_barrier((mid, near, ring_a))
    near = row_near(near)
    end = row_far(light(row_mid_kernel, "row_mid", (block16,), 8, stay, mid)[0])
    *came, near, end = lax.optimization_barrier((*came, near, end))
    own_a, a1, a2, a3, own_b, b1, b2, b3 = weight_call(0, where, held, delta, came)
    came = (y_forth(a1), y_across(a2), y_back(a3), x_forth(b1), x_across(b2), x_back(b3))
    part = jax.ShapeDtypeStruct((128, width), F32)
    part16 = jax.ShapeDtypeStruct((128, width), BF16)
    stay, leave = light(
        shard_kernel, "shard", (part, part16), 10, where, own_a, *came[:3], own_b, *came[3:], scalars=1,
    )
    weight_grad = light(
        functools.partial(weight_out_kernel, tok), "weight_out", (part16,), 8, stay, z_swap(leave)
    )[0]
    row_grad = light(row_out_kernel, "row_out", (block16,), 8, own_rows, near, end)[0]
    return row_grad, weight_grad


def solution(mesh):
    placed = (P(("dp", "tensor"), None), P(None, "tensor"), P("dp", "tensor"), P("dp"), P("dp"))
    return jax.shard_map(
        on_device,
        mesh=mesh,
        in_specs=placed,
        out_specs=(P(("dp", "tensor"), None), P("dp", "tensor")),
        check_vma=False,
    )
```

```python
import functools

import jax
import jax.numpy as jnp
from jax import lax
from jax.experimental import pallas as pl
from jax.experimental.pallas import tpu as pltpu
from jax.sharding import PartitionSpec as P

TW = 9216
META = 128
F32, BF16 = jnp.float32, jnp.bfloat16


def params(mib):
    return pltpu.CompilerParams(vmem_limit_bytes=mib << 20)


LIGHT = pl.CostEstimate(flops=0, bytes_accessed=0, transcendentals=0)


def iota(shape, axis):
    return lax.broadcasted_iota(jnp.int32, shape, axis)


def column(row):
    return jnp.broadcast_to(row.astype(F32), (META, row.shape[1])).T


def as_row(col):
    return jnp.broadcast_to(col, (col.shape[0], META)).T[:1]


def scale_of(exps):
    return jnp.where(exps > 0.5, 2.0, jnp.where(exps < -0.5, 0.5, 1.0))


def squares_kernel(exps_ref, rows_ref, squares_ref):
    rows = rows_ref[...].astype(F32)
    scale = scale_of(exps_ref[...].astype(F32))
    squares_ref[...] = as_row(jnp.sum(rows * rows, axis=1, keepdims=True)) * (scale * scale)


def sum_kernel(*refs):
    total = refs[0][...]
    for ref in refs[1:-1]:
        total = total + ref[...]
    refs[-1][...] = total


def pack_kernel(share, where_ref, packing_ref, exps_ref, s0_ref, s1_ref, s2_ref, s3_ref, rows_ref, keep_ref, leave_ref):
    tok, width = rows_ref.shape
    packing = packing_ref[...]
    peer = packing // tok
    slot = packing % tok
    plane = tok // share // 2
    peer = jnp.where(peer // plane == where_ref[0], 0, plane) + peer % plane
    earlier = iota((tok, tok), 0) < iota((tok, tok), 1)
    same = (column(peer)[:, :1] == peer.astype(F32)) & earlier
    rank = jnp.sum(jnp.where(same, 1.0, 0.0), axis=0, keepdims=True)
    place = peer * share + rank.astype(jnp.int32)
    pick = jnp.where(iota((tok, tok), 0) == place, 1.0, 0.0).astype(BF16)
    lane = iota((tok, META), 1)
    meta = jnp.where(lane == 0, column(slot // 16), 0.0)
    meta = jnp.where(lane == 1, column(slot % 16), meta)
    meta = jnp.where(lane == 2, column(exps_ref[...]), meta)
    rest = column(s0_ref[...] + s1_ref[...] + s2_ref[...] + s3_ref[...])
    for k in range(3):
        term = rest.astype(BF16).astype(F32)
        meta = jnp.where(lane == 3 + k, term, meta)
        rest = rest - term
    rows = jnp.dot(pick, rows_ref[...], preferred_element_type=F32).astype(BF16)
    meta = jnp.dot(pick, meta.astype(BF16), preferred_element_type=F32).astype(BF16)
    half = tok // 2
    for out_ref, at in ((keep_ref, 0), (leave_ref, half)):
        out_ref[:, :width] = rows[at : at + half]
        out_ref[:, width:] = meta[at : at + half]


def merge_kernel(share, keep_ref, came_ref, out_ref):
    for side, rows_ref in enumerate((keep_ref, came_ref)):
        for peer in range(rows_ref.shape[0] // share):
            out_ref[peer, side * share : (side + 1) * share, :] = rows_ref[peer * share : (peer + 1) * share, :]


def place_kernel(got_ref, target_ref, energy_ref):
    tok, width = target_ref.shape
    meta = got_ref[:, width:].astype(F32).T
    slot = (meta[0:1] * 16.0 + meta[1:2]).astype(jnp.int32)
    here = iota((tok, tok), 0) == slot
    pick = jnp.where(here, 1.0, 0.0).astype(BF16)

    def placed(row):
        return jnp.sum(jnp.where(here, row, 0.0), axis=1, keepdims=True)

    rows = jnp.dot(pick, got_ref[:, :width], preferred_element_type=F32)
    target_ref[...] = (rows * placed(scale_of(meta[2:3]))).astype(BF16)
    squares = placed(meta[3:4] + meta[4:5] + meta[5:6])
    energy_ref[...] = jnp.broadcast_to(squares / TW + 1e-05, (tok, META))


def project_kernel(own_ref, sib_ref, adapter_ref, out_ref):
    rows = jnp.concatenate([own_ref[...], sib_ref[...]], axis=0)
    out_ref[...] = jnp.dot(rows, adapter_ref[...], preferred_element_type=F32)


def project_call(own, sib, adapter):
    half, depth = own.shape
    width = adapter.shape[1]
    tile = 384
    return pl.pallas_call(
        project_kernel,
        out_shape=jax.ShapeDtypeStruct((2 * half, width), F32),
        grid=(width // tile,),
        in_specs=[
            pl.BlockSpec((half, depth), lambda n: (0, 0)),
            pl.BlockSpec((half, depth), lambda n: (0, 0)),
            pl.BlockSpec((depth, tile), lambda n: (0, n)),
        ],
        out_specs=pl.BlockSpec((2 * half, tile), lambda n: (0, n)),
        compiler_params=params(14),
        cost_estimate=LIGHT,
        name="project",
    )(own, sib, adapter)


def delta_kernel(where_ref, p0_ref, p1_ref, p2_ref, p3_ref, target_ref, energy_ref, delta_ref):
    half = p0_ref.shape[0] // 2
    zh, core = where_ref[3], where_ref[4]
    step = 1 - 2 * core
    for s, p_ref in enumerate((p0_ref, p1_ref, p2_ref, p3_ref)):
        mine = ((zh - step * s + 4) % 4) * 2 + core
        sibs = ((zh + step * s + 4) % 4) * 2 + 1 - core
        for side, block in enumerate((mine, sibs)):
            token = pl.ds(pl.multiple_of(block * half, half), half)
            diff = p_ref[side * half : (side + 1) * half, :] - target_ref[token, :].astype(F32)
            at = (2 * s + side) * half
            delta_ref[at : at + half, :] = (diff / energy_ref[token, :1]).astype(BF16)


def row_kernel(delta_ref, adapter_ref, *refs):
    keeps, send_ref = refs[:4], refs[4]
    half = keeps[0].shape[0]
    term = lax.dot_general(delta_ref[...], adapter_ref[...], (((1,), (1,)), ((), ())), preferred_element_type=F32)
    for s in range(4):
        keeps[s][...] = term[2 * s * half : (2 * s + 1) * half]
        send_ref[s * half : (s + 1) * half, :] = term[(2 * s + 1) * half : (2 * s + 2) * half].astype(BF16)


def row_call(delta, adapter):
    tok, width = delta.shape
    half = tok // 8
    depth = adapter.shape[0]
    tile = 512
    return pl.pallas_call(
        row_kernel,
        out_shape=(jax.ShapeDtypeStruct((half, depth), F32),) * 4 + (jax.ShapeDtypeStruct((4 * half, depth), BF16),),
        grid=(depth // tile,),
        in_specs=[
            pl.BlockSpec((tok, width), lambda n: (0, 0)),
            pl.BlockSpec((tile, width), lambda n: (n, 0)),
        ],
        out_specs=(pl.BlockSpec((half, tile), lambda n: (0, n)),) * 4
        + (pl.BlockSpec((4 * half, tile), lambda n: (0, n)),),
        compiler_params=params(11),
        cost_estimate=LIGHT,
        name="row_terms",
    )(delta, adapter)


def weight_kernel(k, side, with_came, where_ref, *refs):
    hidden, delta = refs[:8], refs[8]
    came = refs[9:11] if with_came else (None, None)
    outs, left = refs[9 + 2 * with_came : -1], refs[-1]
    half = hidden[0].shape[0]
    x, y, core = where_ref[1], where_ref[2], where_ref[4]
    ahead = k * (1 - 2 * core) + 4
    for chunk in range(2):
        for at in range(2):
            j = 2 * side + at
            if chunk == 0:
                block = ((x + ahead) % 4) * 4 + (y + j) % 4
            else:
                block = 16 + ((x + j) % 4) * 4 + (y + ahead) % 4
            columns = pl.ds(pl.multiple_of(block * 128, 128), 128)
            for part in range(8):
                left[part * half : (part + 1) * half, at * 128 : (at + 1) * 128] = hidden[part][:, columns]
        term = lax.dot_general(left[...], delta[...], (((0,), (0,)), ((), ())), preferred_element_type=F32)
        if with_came:
            term = term + came[chunk][...].astype(F32)
        if k == 0:
            for at in range(2):
                out = outs[2 * chunk + at]
                out[...] = term[128 * at : 128 * (at + 1)].astype(out.dtype)
        else:
            outs[chunk][...] = term.astype(BF16)


def weight_call(k, side, where, hidden, delta, came=()):
    tokens = 8 * hidden[0].shape[0]
    width = delta.shape[1]
    vmem = pl.BlockSpec(memory_space=pltpu.VMEM)
    if k == 0:
        kinds = [jax.ShapeDtypeStruct((128, width), BF16 if side else F32), jax.ShapeDtypeStruct((128, width), BF16)]
    else:
        kinds = [jax.ShapeDtypeStruct((256, width), BF16)]
    return pl.pallas_call(
        functools.partial(weight_kernel, k, side, len(came) > 0),
        out_shape=tuple(kinds * 2),
        in_specs=[pl.BlockSpec(memory_space=pltpu.SMEM)] + [vmem] * (9 + len(came)),
        out_specs=(vmem,) * (2 * len(kinds)),
        scratch_shapes=[pltpu.VMEM((tokens, 256), BF16)],
        compiler_params=params(18),
        cost_estimate=LIGHT,
        name=f"weight_{k}_{side}",
    )(where, *hidden, delta, *came)


def light(kernel, name, out_shape, mib, *args, scalars=0):
    vmem = pl.BlockSpec(memory_space=pltpu.VMEM)
    return pl.pallas_call(
        kernel,
        out_shape=tuple(out_shape),
        in_specs=[pl.BlockSpec(memory_space=pltpu.SMEM)] * scalars + [vmem] * (len(args) - scalars),
        out_specs=(vmem,) * len(out_shape),
        compiler_params=params(mib),
        cost_estimate=LIGHT,
        name=name,
    )(*args)


def shard_kernel(where, own_a, a1, a2, a3, own_b, b1, b2, b3, stay, leave):
    sum_a = own_a[...] + a1[...].astype(F32) + a2[...].astype(F32) + a3[...].astype(F32)
    sum_b = own_b[...] + b1[...].astype(F32) + b2[...].astype(F32) + b3[...].astype(F32)
    low = where[0] == 0
    stay[...] = jnp.where(low, sum_a, sum_b)
    leave[...] = jnp.where(low, sum_b, sum_a).astype(BF16)


def weight_out_kernel(tokens, stay, came, out):
    out[...] = ((stay[...] + came[...].astype(F32)) / tokens).astype(BF16)


def row_out_kernel(pair, came, out):
    out[...] = (pair[...] + came[...].astype(F32)).astype(BF16)


def pair_kernel(k0, k1, k2, k3, swapped, *outs):
    half = k0.shape[0]
    for s, keep in enumerate((k0, k1, k2, k3)):
        total = keep[...] + swapped[s * half : (s + 1) * half, :].astype(F32)
        outs[s][...] = total.astype(outs[s].dtype)


def on_device(hidden, adapter, teacher_rows, scale_exps, packing):
    tok, width = teacher_rows.shape
    half = hidden.shape[0]
    peers = lax.axis_size("dp")
    dp, tensor = lax.axis_index("dp"), lax.axis_index("tensor")
    zl, x, y = dp // 16, (dp // 4) % 4, dp % 4
    zh, core = tensor // 2, tensor % 2

    def over_dp(move):
        pairs = []
        for i in range(32):
            a, b, c = move(i // 16, (i // 4) % 4, i % 4)
            pairs.append((i, (a % 2) * 16 + (b % 4) * 4 + c % 4))
        return lambda value: lax.ppermute(value, "dp", pairs)

    def over_tensor(move):
        pairs = []
        for i in range(8):
            a, b = move(i // 2, i % 2)
            pairs.append((i, (a % 4) * 2 + b % 2))
        return lambda value: lax.ppermute(value, "tensor", pairs)

    def by_core(move):
        pairs = []
        for i in range(256):
            d, t = i // 8, i % 8
            b, c = move((d // 4) % 4, d % 4, 1 - 2 * (t % 2))
            pairs.append((i, ((d // 16) * 16 + (b % 4) * 4 + c % 4) * 8 + t))
        return lambda value: lax.ppermute(value, ("dp", "tensor"), pairs)

    x_ring = by_core(lambda b, c, way: (b + way, c))
    y_ring = by_core(lambda b, c, way: (b, c + way))
    x_forth, x_back = over_dp(lambda a, b, c: (a, b + 1, c)), over_dp(lambda a, b, c: (a, b - 1, c))
    y_forth, y_back = over_dp(lambda a, b, c: (a, b, c + 1)), over_dp(lambda a, b, c: (a, b, c - 1))
    x_across, y_across = over_dp(lambda a, b, c: (a, b + 2, c)), over_dp(lambda a, b, c: (a, b, c + 2))
    z_swap = over_dp(lambda a, b, c: (a + 1, b, c))
    core_swap = over_tensor(lambda a, b: (a, b + 1))
    chain = over_tensor(lambda a, b: (a + 1 - 2 * b, b))

    where = jnp.stack([zl, x, y, zh, core]).astype(jnp.int32)
    row = jax.ShapeDtypeStruct((1, tok), F32)
    share = tok // peers
    lanes = width + META
    packing, scale_exps = packing.reshape(1, tok), scale_exps.reshape(1, tok)

    squares = light(squares_kernel, "squares", (row,), 10, scale_exps, teacher_rows)[0]
    squares = light(sum_kernel, "pair_squares", (row,), 4, squares, core_swap(squares))[0]
    others = [over_tensor(lambda a, b, k=k: (a + k, b))(squares) for k in (1, 2, 3)]
    own = [hidden, chain(hidden)]
    own[1], *others = lax.optimization_barrier((own[1], *others))
    half_rows = jax.ShapeDtypeStruct((tok // 2, lanes), BF16)
    keep, leave = light(
        functools.partial(pack_kernel, share), "pack", (half_rows, half_rows), 18,
        where, packing, scale_exps, squares, *others, teacher_rows, scalars=1,
    )
    came = z_swap(leave)
    own.append(chain(own[1]))
    sib = [core_swap(block) for block in own]
    projected = [project_call(own[s], sib[s], adapter) for s in range(3)]
    came, *projected[:2] = lax.optimization_barrier((came, *projected[:2]))
    own.append(chain(own[2]))
    own[3], projected[2] = lax.optimization_barrier((own[3], projected[2]))
    sib.append(core_swap(own[3]))
    projected.append(project_call(own[3], sib[3], adapter))
    merged = light(
        functools.partial(merge_kernel, share), "merge",
        (jax.ShapeDtypeStruct((peers // 2, 2 * share, lanes), BF16),), 10, keep, came,
    )[0]
    groups = [list(range(peers // 2)), list(range(peers // 2, peers))]
    got = lax.all_to_all(merged, "dp", 0, 0, axis_index_groups=groups, tiled=True)
    got, *projected[2:] = lax.optimization_barrier((got, *projected[2:]))
    target, energy = light(
        place_kernel, "place",
        (jax.ShapeDtypeStruct((tok, width), BF16), jax.ShapeDtypeStruct((tok, META), F32)), 16,
        got.reshape(tok, lanes),
    )
    delta = light(
        delta_kernel, "delta", (jax.ShapeDtypeStruct((tok, width), BF16),), 12,
        where, *projected, target, energy, scalars=1,
    )[0]

    held = [part for pair in zip(own, sib) for part in pair]
    def step(k, side, given, came=()):
        ring_a, ring_b = weight_call(k, side, where, held, given, came)
        return ring_a, (x_ring(ring_a), y_ring(ring_b))

    mark, came_0 = step(3, 0, delta)
    later, _ = lax.optimization_barrier((delta, mark))
    mark, came_1 = step(3, 1, later)
    later, _ = lax.optimization_barrier((delta, mark))
    *keeps, send = row_call(later, adapter)
    *came_0, send = lax.optimization_barrier((*came_0, send))
    mark, came_0 = step(2, 0, delta, came_0)
    *came_1, _ = lax.optimization_barrier((*came_1, mark))
    mark, came_1 = step(2, 1, delta, came_1)
    send, _ = lax.optimization_barrier((send, mark))
    swapped = core_swap(send)
    block = jax.ShapeDtypeStruct((half, hidden.shape[1]), F32)
    block16 = jax.ShapeDtypeStruct(block.shape, BF16)
    pair = light(pair_kernel, "pair", (block, block16, block, block), 14, *keeps, swapped)
    total = chain(pair[1])
    *came_0, _ = lax.optimization_barrier((*came_0, pair[1]))
    mark, came_0 = step(1, 0, delta, came_0)
    *came_1, total, _ = lax.optimization_barrier((*came_1, total, mark))
    mark, came_1 = step(1, 1, delta, came_1)
    total, _ = lax.optimization_barrier((total, mark))
    total = chain(light(row_out_kernel, "row_2", (block16,), 8, pair[2], total)[0])
    own_a, a1, own_b, b1 = weight_call(0, 0, where, held, delta, came_0)
    came = [y_forth(a1), x_forth(b1)]
    *came_1, total, _ = lax.optimization_barrier((*came_1, total, a1))
    a2, a3, b2, b3 = weight_call(0, 1, where, held, delta, came_1)
    total, _ = lax.optimization_barrier((total, a2))
    total = chain(light(row_out_kernel, "row_3", (block16,), 8, pair[3], total)[0])
    came = (came[0], y_across(a2), y_back(a3), came[1], x_across(b2), x_back(b3))
    *came, total = lax.optimization_barrier((*came, total))
    part = jax.ShapeDtypeStruct((128, width), F32)
    part16 = jax.ShapeDtypeStruct((128, width), BF16)
    stay, leave = light(
        shard_kernel, "shard", (part, part16), 10, where, own_a, *came[:3], own_b, *came[3:], scalars=1,
    )
    weight_grad = light(
        functools.partial(weight_out_kernel, tok), "weight_out", (part16,), 8, stay, z_swap(leave)
    )[0]
    row_grad = light(row_out_kernel, "row_0", (block16,), 8, pair[0], total)[0]
    return row_grad, weight_grad


def solution(mesh):
    placed = (P(("dp", "tensor"), None), P(None, "tensor"), P("dp", "tensor"), P("dp"), P("dp"))
    return jax.shard_map(
        on_device,
        mesh=mesh,
        in_specs=placed,
        out_specs=(P(("dp", "tensor"), None), P("dp", "tensor")),
        check_vma=False,
    )
```

```python
import functools

import jax
import jax.numpy as jnp
from jax import lax
from jax.experimental import pallas as pl
from jax.experimental.pallas import tpu as pltpu
from jax.sharding import PartitionSpec as P

TW = 9216
META = 128
F32, BF16 = jnp.float32, jnp.bfloat16


def params(mib):
    return pltpu.CompilerParams(vmem_limit_bytes=mib << 20)


LIGHT = pl.CostEstimate(flops=0, bytes_accessed=0, transcendentals=0)


def iota(shape, axis):
    return lax.broadcasted_iota(jnp.int32, shape, axis)


def column(row):
    return jnp.broadcast_to(row.astype(F32), (META, row.shape[1])).T


def as_row(col):
    return jnp.broadcast_to(col, (col.shape[0], META)).T[:1]


def scale_of(exps):
    return jnp.where(exps > 0.5, 2.0, jnp.where(exps < -0.5, 0.5, 1.0))


def squares_kernel(exps_ref, rows_ref, squares_ref):
    rows = rows_ref[...].astype(F32)
    scale = scale_of(exps_ref[...].astype(F32))
    squares_ref[...] = as_row(jnp.sum(rows * rows, axis=1, keepdims=True)) * (scale * scale)


def sum_kernel(*refs):
    total = refs[0][...]
    for ref in refs[1:-1]:
        total = total + ref[...]
    refs[-1][...] = total


def pack_kernel(share, where_ref, packing_ref, exps_ref, s0_ref, s1_ref, s2_ref, s3_ref, rows_ref, keep_ref, leave_ref):
    tok, width = rows_ref.shape
    packing = packing_ref[...]
    peer = packing // tok
    slot = packing % tok
    plane = tok // share // 2
    peer = jnp.where(peer // plane == where_ref[0], 0, plane) + peer % plane
    earlier = iota((tok, tok), 0) < iota((tok, tok), 1)
    same = (column(peer)[:, :1] == peer.astype(F32)) & earlier
    rank = jnp.sum(jnp.where(same, 1.0, 0.0), axis=0, keepdims=True)
    place = peer * share + rank.astype(jnp.int32)
    pick = jnp.where(iota((tok, tok), 0) == place, 1.0, 0.0).astype(BF16)
    lane = iota((tok, META), 1)
    meta = jnp.where(lane == 0, column(slot // 16), 0.0)
    meta = jnp.where(lane == 1, column(slot % 16), meta)
    meta = jnp.where(lane == 2, column(exps_ref[...]), meta)
    rest = column(s0_ref[...] + s1_ref[...] + s2_ref[...] + s3_ref[...])
    for k in range(3):
        term = rest.astype(BF16).astype(F32)
        meta = jnp.where(lane == 3 + k, term, meta)
        rest = rest - term
    rows = jnp.dot(pick, rows_ref[...], preferred_element_type=F32).astype(BF16)
    meta = jnp.dot(pick, meta.astype(BF16), preferred_element_type=F32).astype(BF16)
    half = tok // 2
    for out_ref, at in ((keep_ref, 0), (leave_ref, half)):
        out_ref[:, :width] = rows[at : at + half]
        out_ref[:, width:] = meta[at : at + half]


def merge_kernel(share, keep_ref, came_ref, out_ref):
    for side, rows_ref in enumerate((keep_ref, came_ref)):
        for peer in range(rows_ref.shape[0] // share):
            out_ref[peer, side * share : (side + 1) * share, :] = rows_ref[peer * share : (peer + 1) * share, :]


def place_kernel(got_ref, target_ref, energy_ref):
    tok, width = target_ref.shape
    meta = got_ref[:, width:].astype(F32).T
    slot = (meta[0:1] * 16.0 + meta[1:2]).astype(jnp.int32)
    here = iota((tok, tok), 0) == slot
    pick = jnp.where(here, 1.0, 0.0).astype(BF16)

    def placed(row):
        return jnp.sum(jnp.where(here, row, 0.0), axis=1, keepdims=True)

    rows = jnp.dot(pick, got_ref[:, :width], preferred_element_type=F32)
    target_ref[...] = (rows * placed(scale_of(meta[2:3]))).astype(BF16)
    squares = placed(meta[3:4] + meta[4:5] + meta[5:6])
    energy_ref[...] = jnp.broadcast_to(squares / TW + 1e-05, (tok, META))


def project_kernel(own_ref, sib_ref, adapter_ref, out_ref):
    rows = jnp.concatenate([own_ref[...], sib_ref[...]], axis=0)
    out_ref[...] = jnp.dot(rows, adapter_ref[...], preferred_element_type=F32)


def project_call(own, sib, adapter):
    half, depth = own.shape
    width = adapter.shape[1]
    tile = 384
    return pl.pallas_call(
        project_kernel,
        out_shape=jax.ShapeDtypeStruct((2 * half, width), F32),
        grid=(width // tile,),
        in_specs=[
            pl.BlockSpec((half, depth), lambda n: (0, 0)),
            pl.BlockSpec((half, depth), lambda n: (0, 0)),
            pl.BlockSpec((depth, tile), lambda n: (0, n)),
        ],
        out_specs=pl.BlockSpec((2 * half, tile), lambda n: (0, n)),
        compiler_params=params(14),
        cost_estimate=LIGHT,
        name="project",
    )(own, sib, adapter)


def delta_kernel(where_ref, p0_ref, p1_ref, p2_ref, p3_ref, target_ref, energy_ref, delta_ref):
    half = p0_ref.shape[0] // 2
    zh, core = where_ref[3], where_ref[4]
    step = 1 - 2 * core
    for s, p_ref in enumerate((p0_ref, p1_ref, p2_ref, p3_ref)):
        mine = ((zh - step * s + 4) % 4) * 2 + core
        sibs = ((zh + step * s + 4) % 4) * 2 + 1 - core
        for side, block in enumerate((mine, sibs)):
            token = pl.ds(pl.multiple_of(block * half, half), half)
            diff = p_ref[side * half : (side + 1) * half, :] - target_ref[token, :].astype(F32)
            at = (2 * s + side) * half
            delta_ref[at : at + half, :] = (diff / energy_ref[token, :1]).astype(BF16)


def row_kernel(delta_ref, adapter_ref, *refs):
    keeps, send_ref = refs[:4], refs[4]
    half = keeps[0].shape[0]
    term = lax.dot_general(delta_ref[...], adapter_ref[...], (((1,), (1,)), ((), ())), preferred_element_type=F32)
    for s in range(4):
        keeps[s][...] = term[2 * s * half : (2 * s + 1) * half]
        send_ref[s * half : (s + 1) * half, :] = term[(2 * s + 1) * half : (2 * s + 2) * half].astype(BF16)


def row_call(delta, adapter):
    tok, width = delta.shape
    half = tok // 8
    depth = adapter.shape[0]
    tile = 512
    return pl.pallas_call(
        row_kernel,
        out_shape=(jax.ShapeDtypeStruct((half, depth), F32),) * 4 + (jax.ShapeDtypeStruct((4 * half, depth), BF16),),
        grid=(depth // tile,),
        in_specs=[
            pl.BlockSpec((tok, width), lambda n: (0, 0)),
            pl.BlockSpec((tile, width), lambda n: (n, 0)),
        ],
        out_specs=(pl.BlockSpec((half, tile), lambda n: (0, n)),) * 4
        + (pl.BlockSpec((4 * half, tile), lambda n: (0, n)),),
        compiler_params=params(11),
        cost_estimate=LIGHT,
        name="row_terms",
    )(delta, adapter)


def weight_kernel(k, side, with_came, where_ref, *refs):
    hidden, delta = refs[:8], refs[8]
    came = refs[9:11] if with_came else (None, None)
    outs, left = refs[9 + 2 * with_came : -1], refs[-1]
    half = hidden[0].shape[0]
    x, y, core = where_ref[1], where_ref[2], where_ref[4]
    ahead = k * (1 - 2 * core) + 4
    for chunk in range(2):
        for at in range(2):
            j = 2 * side + at
            if chunk == 0:
                block = ((x + ahead) % 4) * 4 + (y + j) % 4
            else:
                block = 16 + ((x + j) % 4) * 4 + (y + ahead) % 4
            columns = pl.ds(pl.multiple_of(block * 128, 128), 128)
            for part in range(8):
                left[part * half : (part + 1) * half, at * 128 : (at + 1) * 128] = hidden[part][:, columns]
        term = lax.dot_general(left[...], delta[...], (((0,), (0,)), ((), ())), preferred_element_type=F32)
        if with_came:
            term = term + came[chunk][...].astype(F32)
        if k == 0:
            for at in range(2):
                out = outs[2 * chunk + at]
                out[...] = term[128 * at : 128 * (at + 1)].astype(out.dtype)
        else:
            outs[chunk][...] = term.astype(BF16)


def weight_call(k, side, where, hidden, delta, came=()):
    tokens = 8 * hidden[0].shape[0]
    width = delta.shape[1]
    vmem = pl.BlockSpec(memory_space=pltpu.VMEM)
    if k == 0:
        kinds = [jax.ShapeDtypeStruct((128, width), BF16 if side else F32), jax.ShapeDtypeStruct((128, width), BF16)]
    else:
        kinds = [jax.ShapeDtypeStruct((256, width), BF16)]
    return pl.pallas_call(
        functools.partial(weight_kernel, k, side, len(came) > 0),
        out_shape=tuple(kinds * 2),
        in_specs=[pl.BlockSpec(memory_space=pltpu.SMEM)] + [vmem] * (9 + len(came)),
        out_specs=(vmem,) * (2 * len(kinds)),
        scratch_shapes=[pltpu.VMEM((tokens, 256), BF16)],
        compiler_params=params(18),
        cost_estimate=LIGHT,
        name=f"weight_{k}_{side}",
    )(where, *hidden, delta, *came)


def light(kernel, name, out_shape, mib, *args, scalars=0):
    vmem = pl.BlockSpec(memory_space=pltpu.VMEM)
    return pl.pallas_call(
        kernel,
        out_shape=tuple(out_shape),
        in_specs=[pl.BlockSpec(memory_space=pltpu.SMEM)] * scalars + [vmem] * (len(args) - scalars),
        out_specs=(vmem,) * len(out_shape),
        compiler_params=params(mib),
        cost_estimate=LIGHT,
        name=name,
    )(*args)


def shard_kernel(where, own_a, a1, a2, a3, own_b, b1, b2, b3, stay, leave):
    sum_a = own_a[...] + a1[...].astype(F32) + a2[...].astype(F32) + a3[...].astype(F32)
    sum_b = own_b[...] + b1[...].astype(F32) + b2[...].astype(F32) + b3[...].astype(F32)
    low = where[0] == 0
    stay[...] = jnp.where(low, sum_a, sum_b)
    leave[...] = jnp.where(low, sum_b, sum_a).astype(BF16)


def weight_out_kernel(tokens, stay, came, out):
    out[...] = ((stay[...] + came[...].astype(F32)) / tokens).astype(BF16)


def row_out_kernel(pair, came, out):
    out[...] = (pair[...] + came[...].astype(F32)).astype(BF16)


def pair_kernel(k0, k1, k2, k3, swapped, *outs):
    half = k0.shape[0]
    for s, keep in enumerate((k0, k1, k2, k3)):
        total = keep[...] + swapped[s * half : (s + 1) * half, :].astype(F32)
        outs[s][...] = total.astype(outs[s].dtype)


def on_device(hidden, adapter, teacher_rows, scale_exps, packing):
    tok, width = teacher_rows.shape
    half = hidden.shape[0]
    peers = lax.axis_size("dp")
    dp, tensor = lax.axis_index("dp"), lax.axis_index("tensor")
    zl, x, y = dp // 16, (dp // 4) % 4, dp % 4
    zh, core = tensor // 2, tensor % 2

    def over_dp(move):
        pairs = []
        for i in range(32):
            a, b, c = move(i // 16, (i // 4) % 4, i % 4)
            pairs.append((i, (a % 2) * 16 + (b % 4) * 4 + c % 4))
        return lambda value: lax.ppermute(value, "dp", pairs)

    def over_tensor(move):
        pairs = []
        for i in range(8):
            a, b = move(i // 2, i % 2)
            pairs.append((i, (a % 4) * 2 + b % 2))
        return lambda value: lax.ppermute(value, "tensor", pairs)

    def by_core(move):
        pairs = []
        for i in range(256):
            d, t = i // 8, i % 8
            b, c = move((d // 4) % 4, d % 4, 1 - 2 * (t % 2))
            pairs.append((i, ((d // 16) * 16 + (b % 4) * 4 + c % 4) * 8 + t))
        return lambda value: lax.ppermute(value, ("dp", "tensor"), pairs)

    x_ring = by_core(lambda b, c, way: (b + way, c))
    y_ring = by_core(lambda b, c, way: (b, c + way))
    x_forth, x_back = over_dp(lambda a, b, c: (a, b + 1, c)), over_dp(lambda a, b, c: (a, b - 1, c))
    y_forth, y_back = over_dp(lambda a, b, c: (a, b, c + 1)), over_dp(lambda a, b, c: (a, b, c - 1))
    x_across, y_across = over_dp(lambda a, b, c: (a, b + 2, c)), over_dp(lambda a, b, c: (a, b, c + 2))
    z_swap = over_dp(lambda a, b, c: (a + 1, b, c))
    core_swap = over_tensor(lambda a, b: (a, b + 1))
    chain = over_tensor(lambda a, b: (a + 1 - 2 * b, b))

    where = jnp.stack([zl, x, y, zh, core]).astype(jnp.int32)
    row = jax.ShapeDtypeStruct((1, tok), F32)
    share = tok // peers
    lanes = width + META
    packing, scale_exps = packing.reshape(1, tok), scale_exps.reshape(1, tok)

    squares = light(squares_kernel, "squares", (row,), 10, scale_exps, teacher_rows)[0]
    squares = light(sum_kernel, "pair_squares", (row,), 4, squares, core_swap(squares))[0]
    others = [over_tensor(lambda a, b, k=k: (a + k, b))(squares) for k in (1, 2, 3)]
    own = [hidden, chain(hidden)]
    own[1], *others = lax.optimization_barrier((own[1], *others))
    half_rows = jax.ShapeDtypeStruct((tok // 2, lanes), BF16)
    keep, leave = light(
        functools.partial(pack_kernel, share), "pack", (half_rows, half_rows), 18,
        where, packing, scale_exps, squares, *others, teacher_rows, scalars=1,
    )
    came = z_swap(leave)
    own.append(chain(own[1]))
    sib = [core_swap(block) for block in own]
    projected = [project_call(own[s], sib[s], adapter) for s in range(3)]
    came, *projected[:2] = lax.optimization_barrier((came, *projected[:2]))
    own.append(chain(own[2]))
    own[3], projected[2] = lax.optimization_barrier((own[3], projected[2]))
    sib.append(core_swap(own[3]))
    projected.append(project_call(own[3], sib[3], adapter))
    merged = light(
        functools.partial(merge_kernel, share), "merge",
        (jax.ShapeDtypeStruct((peers // 2, 2 * share, lanes), BF16),), 10, keep, came,
    )[0]
    groups = [list(range(peers // 2)), list(range(peers // 2, peers))]
    got = lax.all_to_all(merged, "dp", 0, 0, axis_index_groups=groups, tiled=True)
    got, *projected[2:] = lax.optimization_barrier((got, *projected[2:]))
    target, energy = light(
        place_kernel, "place",
        (jax.ShapeDtypeStruct((tok, width), BF16), jax.ShapeDtypeStruct((tok, META), F32)), 16,
        got.reshape(tok, lanes),
    )
    delta = light(
        delta_kernel, "delta", (jax.ShapeDtypeStruct((tok, width), BF16),), 12,
        where, *projected, target, energy, scalars=1,
    )[0]

    held = [part for pair in zip(own, sib) for part in pair]
    def step(k, side, given, came=()):
        ring_a, ring_b = weight_call(k, side, where, held, given, came)
        return ring_a, (x_ring(ring_a), y_ring(ring_b))

    mark, came_0 = step(3, 0, delta)
    later, _ = lax.optimization_barrier((delta, mark))
    mark, came_1 = step(3, 1, later)
    later, _ = lax.optimization_barrier((delta, mark))
    *keeps, send = row_call(later, adapter)
    *came_0, send = lax.optimization_barrier((*came_0, send))
    mark, came_0 = step(2, 0, delta, came_0)
    *came_1, _ = lax.optimization_barrier((*came_1, mark))
    mark, came_1 = step(2, 1, delta, came_1)
    send, _ = lax.optimization_barrier((send, mark))
    swapped = core_swap(send)
    block = jax.ShapeDtypeStruct((half, hidden.shape[1]), F32)
    block16 = jax.ShapeDtypeStruct(block.shape, BF16)
    pair = light(pair_kernel, "pair", (block, block16, block, block), 14, *keeps, swapped)
    total = chain(pair[1])
    *came_0, _ = lax.optimization_barrier((*came_0, pair[1]))
    mark, came_0 = step(1, 0, delta, came_0)
    *came_1, _ = lax.optimization_barrier((*came_1, mark))
    mark, came_1 = step(1, 1, delta, came_1)
    total, _ = lax.optimization_barrier((total, mark))
    sent = light(row_out_kernel, "row_2", (block16,), 8, pair[2], total)[0]
    total = chain(sent)
    *came_0, _ = lax.optimization_barrier((*came_0, sent))
    own_a, a1, own_b, b1 = weight_call(0, 0, where, held, delta, came_0)
    came = [y_forth(a1), x_forth(b1)]
    *came_1, total, _ = lax.optimization_barrier((*came_1, total, a1))
    a2, a3, b2, b3 = weight_call(0, 1, where, held, delta, came_1)
    total, _ = lax.optimization_barrier((total, a2))
    total = chain(light(row_out_kernel, "row_3", (block16,), 8, pair[3], total)[0])
    came = (came[0], y_across(a2), y_back(a3), came[1], x_across(b2), x_back(b3))
    *came, total = lax.optimization_barrier((*came, total))
    part = jax.ShapeDtypeStruct((128, width), F32)
    part16 = jax.ShapeDtypeStruct((128, width), BF16)
    stay, leave = light(
        shard_kernel, "shard", (part, part16), 10, where, own_a, *came[:3], own_b, *came[3:], scalars=1,
    )
    weight_grad = light(
        functools.partial(weight_out_kernel, tok), "weight_out", (part16,), 8, stay, z_swap(leave)
    )[0]
    row_grad = light(row_out_kernel, "row_0", (block16,), 8, pair[0], total)[0]
    return row_grad, weight_grad


def solution(mesh):
    placed = (P(("dp", "tensor"), None), P(None, "tensor"), P("dp", "tensor"), P("dp"), P("dp"))
    return jax.shard_map(
        on_device,
        mesh=mesh,
        in_specs=placed,
        out_specs=(P(("dp", "tensor"), None), P("dp", "tensor")),
        check_vma=False,
    )
```

```python
import functools

import jax
import jax.numpy as jnp
from jax import lax
from jax.experimental import pallas as pl
from jax.experimental.pallas import tpu as pltpu
from jax.sharding import PartitionSpec as P

TW = 9216
META = 128
F32, BF16 = jnp.float32, jnp.bfloat16


def params(mib):
    return pltpu.CompilerParams(vmem_limit_bytes=mib << 20)


LIGHT = pl.CostEstimate(flops=0, bytes_accessed=0, transcendentals=0)


def iota(shape, axis):
    return lax.broadcasted_iota(jnp.int32, shape, axis)


def column(row):
    return jnp.broadcast_to(row.astype(F32), (META, row.shape[1])).T


def as_row(col):
    return jnp.broadcast_to(col, (col.shape[0], META)).T[:1]


def scale_of(exps):
    return jnp.where(exps > 0.5, 2.0, jnp.where(exps < -0.5, 0.5, 1.0))


def squares_kernel(exps_ref, rows_ref, squares_ref):
    rows = rows_ref[...].astype(F32)
    scale = scale_of(exps_ref[...].astype(F32))
    squares_ref[...] = as_row(jnp.sum(rows * rows, axis=1, keepdims=True)) * (scale * scale)


def sum_kernel(*refs):
    total = refs[0][...]
    for ref in refs[1:-1]:
        total = total + ref[...]
    refs[-1][...] = total


def pack_kernel(share, where_ref, packing_ref, exps_ref, s0_ref, s1_ref, s2_ref, s3_ref, rows_ref, keep_ref, leave_ref):
    tok, width = rows_ref.shape
    packing = packing_ref[...]
    peer = packing // tok
    slot = packing % tok
    plane = tok // share // 2
    peer = jnp.where(peer // plane == where_ref[0], 0, plane) + peer % plane
    earlier = iota((tok, tok), 0) < iota((tok, tok), 1)
    same = (column(peer)[:, :1] == peer.astype(F32)) & earlier
    rank = jnp.sum(jnp.where(same, 1.0, 0.0), axis=0, keepdims=True)
    place = peer * share + rank.astype(jnp.int32)
    pick = jnp.where(iota((tok, tok), 0) == place, 1.0, 0.0).astype(BF16)
    lane = iota((tok, META), 1)
    meta = jnp.where(lane == 0, column(slot // 16), 0.0)
    meta = jnp.where(lane == 1, column(slot % 16), meta)
    meta = jnp.where(lane == 2, column(exps_ref[...]), meta)
    rest = column(s0_ref[...] + s1_ref[...] + s2_ref[...] + s3_ref[...])
    for k in range(3):
        term = rest.astype(BF16).astype(F32)
        meta = jnp.where(lane == 3 + k, term, meta)
        rest = rest - term
    rows = jnp.dot(pick, rows_ref[...], preferred_element_type=F32).astype(BF16)
    meta = jnp.dot(pick, meta.astype(BF16), preferred_element_type=F32).astype(BF16)
    half = tok // 2
    for out_ref, at in ((keep_ref, 0), (leave_ref, half)):
        out_ref[:, :width] = rows[at : at + half]
        out_ref[:, width:] = meta[at : at + half]


def merge_kernel(share, keep_ref, came_ref, out_ref):
    for side, rows_ref in enumerate((keep_ref, came_ref)):
        for peer in range(rows_ref.shape[0] // share):
            out_ref[peer, side * share : (side + 1) * share, :] = rows_ref[peer * share : (peer + 1) * share, :]


def place_kernel(got_ref, target_ref, energy_ref):
    tok, width = target_ref.shape
    meta = got_ref[:, width:].astype(F32).T
    slot = (meta[0:1] * 16.0 + meta[1:2]).astype(jnp.int32)
    here = iota((tok, tok), 0) == slot
    pick = jnp.where(here, 1.0, 0.0).astype(BF16)

    def placed(row):
        return jnp.sum(jnp.where(here, row, 0.0), axis=1, keepdims=True)

    rows = jnp.dot(pick, got_ref[:, :width], preferred_element_type=F32)
    target_ref[...] = (rows * placed(scale_of(meta[2:3]))).astype(BF16)
    squares = placed(meta[3:4] + meta[4:5] + meta[5:6])
    energy_ref[...] = jnp.broadcast_to(squares / TW + 1e-05, (tok, META))


def project_kernel(own_ref, sib_ref, adapter_ref, out_ref):
    rows = jnp.concatenate([own_ref[...], sib_ref[...]], axis=0)
    out_ref[...] = jnp.dot(rows, adapter_ref[...], preferred_element_type=F32)


def project_call(own, sib, adapter):
    half, depth = own.shape
    width = adapter.shape[1]
    tile = 384
    return pl.pallas_call(
        project_kernel,
        out_shape=jax.ShapeDtypeStruct((2 * half, width), F32),
        grid=(width // tile,),
        in_specs=[
            pl.BlockSpec((half, depth), lambda n: (0, 0)),
            pl.BlockSpec((half, depth), lambda n: (0, 0)),
            pl.BlockSpec((depth, tile), lambda n: (0, n)),
        ],
        out_specs=pl.BlockSpec((2 * half, tile), lambda n: (0, n)),
        compiler_params=params(14),
        cost_estimate=LIGHT,
        name="project",
    )(own, sib, adapter)


def delta_kernel(where_ref, p0_ref, p1_ref, p2_ref, p3_ref, target_ref, energy_ref, delta_ref):
    half = p0_ref.shape[0] // 2
    zh, core = where_ref[3], where_ref[4]
    step = 1 - 2 * core
    for s, p_ref in enumerate((p0_ref, p1_ref, p2_ref, p3_ref)):
        mine = ((zh - step * s + 4) % 4) * 2 + core
        sibs = ((zh + step * s + 4) % 4) * 2 + 1 - core
        for side, block in enumerate((mine, sibs)):
            token = pl.ds(pl.multiple_of(block * half, half), half)
            diff = p_ref[side * half : (side + 1) * half, :] - target_ref[token, :].astype(F32)
            at = (2 * s + side) * half
            delta_ref[at : at + half, :] = (diff / energy_ref[token, :1]).astype(BF16)


def row_kernel(delta_ref, adapter_ref, *refs):
    keeps, send_ref = refs[:4], refs[4]
    half = keeps[0].shape[0]
    term = lax.dot_general(delta_ref[...], adapter_ref[...], (((1,), (1,)), ((), ())), preferred_element_type=F32)
    for s in range(4):
        keeps[s][...] = term[2 * s * half : (2 * s + 1) * half]
        send_ref[s * half : (s + 1) * half, :] = term[(2 * s + 1) * half : (2 * s + 2) * half].astype(BF16)


def row_call(delta, adapter):
    tok, width = delta.shape
    half = tok // 8
    depth = adapter.shape[0]
    tile = 512
    return pl.pallas_call(
        row_kernel,
        out_shape=(jax.ShapeDtypeStruct((half, depth), F32),) * 4 + (jax.ShapeDtypeStruct((4 * half, depth), BF16),),
        grid=(depth // tile,),
        in_specs=[
            pl.BlockSpec((tok, width), lambda n: (0, 0)),
            pl.BlockSpec((tile, width), lambda n: (n, 0)),
        ],
        out_specs=(pl.BlockSpec((half, tile), lambda n: (0, n)),) * 4
        + (pl.BlockSpec((4 * half, tile), lambda n: (0, n)),),
        compiler_params=params(11),
        cost_estimate=LIGHT,
        name="row_terms",
    )(delta, adapter)


def weight_kernel(k, side, with_came, where_ref, *refs):
    hidden, delta = refs[:8], refs[8]
    came = refs[9:11] if with_came else (None, None)
    outs, left = refs[9 + 2 * with_came : -1], refs[-1]
    half = hidden[0].shape[0]
    x, y, core = where_ref[1], where_ref[2], where_ref[4]
    ahead = k * (1 - 2 * core) + 4
    for chunk in range(2):
        for at in range(2):
            j = 2 * side + at
            if chunk == 0:
                block = ((x + ahead) % 4) * 4 + (y + j) % 4
            else:
                block = 16 + ((x + j) % 4) * 4 + (y + ahead) % 4
            columns = pl.ds(pl.multiple_of(block * 128, 128), 128)
            for part in range(8):
                left[part * half : (part + 1) * half, at * 128 : (at + 1) * 128] = hidden[part][:, columns]
        term = lax.dot_general(left[...], delta[...], (((0,), (0,)), ((), ())), preferred_element_type=F32)
        if with_came:
            term = term + came[chunk][...].astype(F32)
        if k == 0:
            for at in range(2):
                out = outs[2 * chunk + at]
                out[...] = term[128 * at : 128 * (at + 1)].astype(out.dtype)
        else:
            outs[chunk][...] = term.astype(BF16)


def weight_call(k, side, where, hidden, delta, came=()):
    tokens = 8 * hidden[0].shape[0]
    width = delta.shape[1]
    vmem = pl.BlockSpec(memory_space=pltpu.VMEM)
    if k == 0:
        kinds = [jax.ShapeDtypeStruct((128, width), BF16 if side else F32), jax.ShapeDtypeStruct((128, width), BF16)]
    else:
        kinds = [jax.ShapeDtypeStruct((256, width), BF16)]
    return pl.pallas_call(
        functools.partial(weight_kernel, k, side, len(came) > 0),
        out_shape=tuple(kinds * 2),
        in_specs=[pl.BlockSpec(memory_space=pltpu.SMEM)] + [vmem] * (9 + len(came)),
        out_specs=(vmem,) * (2 * len(kinds)),
        scratch_shapes=[pltpu.VMEM((tokens, 256), BF16)],
        compiler_params=params(18),
        cost_estimate=LIGHT,
        name=f"weight_{k}_{side}",
    )(where, *hidden, delta, *came)


def light(kernel, name, out_shape, mib, *args, scalars=0):
    vmem = pl.BlockSpec(memory_space=pltpu.VMEM)
    return pl.pallas_call(
        kernel,
        out_shape=tuple(out_shape),
        in_specs=[pl.BlockSpec(memory_space=pltpu.SMEM)] * scalars + [vmem] * (len(args) - scalars),
        out_specs=(vmem,) * len(out_shape),
        compiler_params=params(mib),
        cost_estimate=LIGHT,
        name=name,
    )(*args)


def shard_kernel(where, own_a, a1, a2, a3, own_b, b1, b2, b3, stay, leave):
    sum_a = own_a[...] + a1[...].astype(F32) + a2[...].astype(F32) + a3[...].astype(F32)
    sum_b = own_b[...] + b1[...].astype(F32) + b2[...].astype(F32) + b3[...].astype(F32)
    low = where[0] == 0
    stay[...] = jnp.where(low, sum_a, sum_b)
    leave[...] = jnp.where(low, sum_b, sum_a).astype(BF16)


def weight_out_kernel(tokens, stay, came, out):
    out[...] = ((stay[...] + came[...].astype(F32)) / tokens).astype(BF16)


def row_out_kernel(pair, came, out):
    out[...] = (pair[...] + came[...].astype(F32)).astype(BF16)


def pair_kernel(k0, k1, k2, k3, swapped, *outs):
    half = k0.shape[0]
    for s, keep in enumerate((k0, k1, k2, k3)):
        total = keep[...] + swapped[s * half : (s + 1) * half, :].astype(F32)
        outs[s][...] = total.astype(outs[s].dtype)


def on_device(hidden, adapter, teacher_rows, scale_exps, packing):
    tok, width = teacher_rows.shape
    half = hidden.shape[0]
    peers = lax.axis_size("dp")
    dp, tensor = lax.axis_index("dp"), lax.axis_index("tensor")
    zl, x, y = dp // 16, (dp // 4) % 4, dp % 4
    zh, core = tensor // 2, tensor % 2

    def over_dp(move):
        pairs = []
        for i in range(32):
            a, b, c = move(i // 16, (i // 4) % 4, i % 4)
            pairs.append((i, (a % 2) * 16 + (b % 4) * 4 + c % 4))
        return lambda value: lax.ppermute(value, "dp", pairs)

    def over_tensor(move):
        pairs = []
        for i in range(8):
            a, b = move(i // 2, i % 2)
            pairs.append((i, (a % 4) * 2 + b % 2))
        return lambda value: lax.ppermute(value, "tensor", pairs)

    def by_core(move):
        pairs = []
        for i in range(256):
            d, t = i // 8, i % 8
            b, c = move((d // 4) % 4, d % 4, 1 - 2 * (t % 2))
            pairs.append((i, ((d // 16) * 16 + (b % 4) * 4 + c % 4) * 8 + t))
        return lambda value: lax.ppermute(value, ("dp", "tensor"), pairs)

    x_ring = by_core(lambda b, c, way: (b + way, c))
    y_ring = by_core(lambda b, c, way: (b, c + way))
    x_forth, x_back = over_dp(lambda a, b, c: (a, b + 1, c)), over_dp(lambda a, b, c: (a, b - 1, c))
    y_forth, y_back = over_dp(lambda a, b, c: (a, b, c + 1)), over_dp(lambda a, b, c: (a, b, c - 1))
    x_across, y_across = over_dp(lambda a, b, c: (a, b + 2, c)), over_dp(lambda a, b, c: (a, b, c + 2))
    z_swap = over_dp(lambda a, b, c: (a + 1, b, c))
    core_swap = over_tensor(lambda a, b: (a, b + 1))
    chain = over_tensor(lambda a, b: (a + 1 - 2 * b, b))

    where = jnp.stack([zl, x, y, zh, core]).astype(jnp.int32)
    row = jax.ShapeDtypeStruct((1, tok), F32)
    share = tok // peers
    lanes = width + META
    packing, scale_exps = packing.reshape(1, tok), scale_exps.reshape(1, tok)

    squares = light(squares_kernel, "squares", (row,), 10, scale_exps, teacher_rows)[0]
    squares = light(sum_kernel, "pair_squares", (row,), 4, squares, core_swap(squares))[0]
    others = [over_tensor(lambda a, b, k=k: (a + k, b))(squares) for k in (1, 2, 3)]
    own = [hidden, chain(hidden)]
    own[1], *others = lax.optimization_barrier((own[1], *others))
    half_rows = jax.ShapeDtypeStruct((tok // 2, lanes), BF16)
    keep, leave = light(
        functools.partial(pack_kernel, share), "pack", (half_rows, half_rows), 18,
        where, packing, scale_exps, squares, *others, teacher_rows, scalars=1,
    )
    came = z_swap(leave)
    own.append(chain(own[1]))
    sib = [core_swap(block) for block in own]
    projected = [project_call(own[s], sib[s], adapter) for s in range(3)]
    came, *projected[:2] = lax.optimization_barrier((came, *projected[:2]))
    own.append(chain(own[2]))
    own[3], projected[2] = lax.optimization_barrier((own[3], projected[2]))
    sib.append(core_swap(own[3]))
    projected.append(project_call(own[3], sib[3], adapter))
    merged = light(
        functools.partial(merge_kernel, share), "merge",
        (jax.ShapeDtypeStruct((peers // 2, 2 * share, lanes), BF16),), 10, keep, came,
    )[0]
    groups = [list(range(peers // 2)), list(range(peers // 2, peers))]
    got = lax.all_to_all(merged, "dp", 0, 0, axis_index_groups=groups, tiled=True)
    got, *projected[2:] = lax.optimization_barrier((got, *projected[2:]))
    target, energy = light(
        place_kernel, "place",
        (jax.ShapeDtypeStruct((tok, width), BF16), jax.ShapeDtypeStruct((tok, META), F32)), 16,
        got.reshape(tok, lanes),
    )
    delta = light(
        delta_kernel, "delta", (jax.ShapeDtypeStruct((tok, width), BF16),), 12,
        where, *projected, target, energy, scalars=1,
    )[0]

    held = [part for pair in zip(own, sib) for part in pair]
    def step(k, side, given, came=()):
        ring_a, ring_b = weight_call(k, side, where, held, given, came)
        return ring_a, (x_ring(ring_a), y_ring(ring_b))

    mark, came_0 = step(3, 0, delta)
    later, _ = lax.optimization_barrier((delta, mark))
    mark, came_1 = step(3, 1, later)
    later, _ = lax.optimization_barrier((delta, mark))
    *keeps, send = row_call(later, adapter)
    *came_0, send = lax.optimization_barrier((*came_0, send))
    mark, came_0 = step(2, 0, delta, came_0)
    *came_1, _ = lax.optimization_barrier((*came_1, mark))
    mark, came_1 = step(2, 1, delta, came_1)
    send, _ = lax.optimization_barrier((send, mark))
    swapped = core_swap(send)
    block = jax.ShapeDtypeStruct((half, hidden.shape[1]), F32)
    block16 = jax.ShapeDtypeStruct(block.shape, BF16)
    pair = light(pair_kernel, "pair", (block, block16, block, block), 14, *keeps, swapped)
    total = chain(pair[1])
    *came_0, _ = lax.optimization_barrier((*came_0, pair[1]))
    mark, came_0 = step(1, 0, delta, came_0)
    *came_1, _ = lax.optimization_barrier((*came_1, mark))
    mark, came_1 = step(1, 1, delta, came_1)
    total, _ = lax.optimization_barrier((total, mark))
    sent = light(row_out_kernel, "row_2", (block16,), 8, pair[2], total)[0]
    total = chain(sent)
    *came_0, _ = lax.optimization_barrier((*came_0, sent))
    own_a, a1, own_b, b1 = weight_call(0, 0, where, held, delta, came_0)
    came = [y_forth(a1), x_forth(b1)]
    *came_1, _ = lax.optimization_barrier((*came_1, a1))
    a2, a3, b2, b3 = weight_call(0, 1, where, held, delta, came_1)
    *came, total, _ = lax.optimization_barrier((*came, total, a2))
    total = chain(light(row_out_kernel, "row_3", (block16,), 8, pair[3], total)[0])
    came = (came[0], y_across(a2), y_back(a3), came[1], x_across(b2), x_back(b3))
    *came, total = lax.optimization_barrier((*came, total))
    part = jax.ShapeDtypeStruct((128, width), F32)
    part16 = jax.ShapeDtypeStruct((128, width), BF16)
    stay, leave = light(
        shard_kernel, "shard", (part, part16), 10, where, own_a, *came[:3], own_b, *came[3:], scalars=1,
    )
    weight_grad = light(
        functools.partial(weight_out_kernel, tok), "weight_out", (part16,), 8, stay, z_swap(leave)
    )[0]
    row_grad = light(row_out_kernel, "row_0", (block16,), 8, pair[0], total)[0]
    return row_grad, weight_grad


def solution(mesh):
    placed = (P(("dp", "tensor"), None), P(None, "tensor"), P("dp", "tensor"), P("dp"), P("dp"))
    return jax.shard_map(
        on_device,
        mesh=mesh,
        in_specs=placed,
        out_specs=(P(("dp", "tensor"), None), P("dp", "tensor")),
        check_vma=False,
    )
```

```python
import functools

import jax
import jax.numpy as jnp
from jax import lax
from jax.experimental import pallas as pl
from jax.experimental.pallas import tpu as pltpu
from jax.sharding import PartitionSpec as P

TW = 9216
META = 128
F32, BF16 = jnp.float32, jnp.bfloat16


def params(mib):
    return pltpu.CompilerParams(vmem_limit_bytes=mib << 20)


LIGHT = pl.CostEstimate(flops=0, bytes_accessed=0, transcendentals=0)


def iota(shape, axis):
    return lax.broadcasted_iota(jnp.int32, shape, axis)


def column(row):
    return jnp.broadcast_to(row.astype(F32), (META, row.shape[1])).T


def as_row(col):
    return jnp.broadcast_to(col, (col.shape[0], META)).T[:1]


def scale_of(exps):
    return jnp.where(exps > 0.5, 2.0, jnp.where(exps < -0.5, 0.5, 1.0))


def squares_kernel(exps_ref, rows_ref, squares_ref):
    rows = rows_ref[...].astype(F32)
    scale = scale_of(exps_ref[...].astype(F32))
    squares_ref[...] = as_row(jnp.sum(rows * rows, axis=1, keepdims=True)) * (scale * scale)


def sum_kernel(*refs):
    total = refs[0][...]
    for ref in refs[1:-1]:
        total = total + ref[...]
    refs[-1][...] = total


def pack_kernel(share, where_ref, packing_ref, exps_ref, s0_ref, s1_ref, s2_ref, s3_ref, rows_ref, keep_ref, leave_ref):
    tok, width = rows_ref.shape
    packing = packing_ref[...]
    peer = packing // tok
    slot = packing % tok
    plane = tok // share // 2
    peer = jnp.where(peer // plane == where_ref[0], 0, plane) + peer % plane
    earlier = iota((tok, tok), 0) < iota((tok, tok), 1)
    same = (column(peer)[:, :1] == peer.astype(F32)) & earlier
    rank = jnp.sum(jnp.where(same, 1.0, 0.0), axis=0, keepdims=True)
    place = peer * share + rank.astype(jnp.int32)
    pick = jnp.where(iota((tok, tok), 0) == place, 1.0, 0.0).astype(BF16)
    lane = iota((tok, META), 1)
    meta = jnp.where(lane == 0, column(slot // 16), 0.0)
    meta = jnp.where(lane == 1, column(slot % 16), meta)
    meta = jnp.where(lane == 2, column(exps_ref[...]), meta)
    rest = column(s0_ref[...] + s1_ref[...] + s2_ref[...] + s3_ref[...])
    for k in range(3):
        term = rest.astype(BF16).astype(F32)
        meta = jnp.where(lane == 3 + k, term, meta)
        rest = rest - term
    rows = jnp.dot(pick, rows_ref[...], preferred_element_type=F32).astype(BF16)
    meta = jnp.dot(pick, meta.astype(BF16), preferred_element_type=F32).astype(BF16)
    half = tok // 2
    for out_ref, at in ((keep_ref, 0), (leave_ref, half)):
        out_ref[:, :width] = rows[at : at + half]
        out_ref[:, width:] = meta[at : at + half]


def merge_kernel(share, keep_ref, came_ref, out_ref):
    for side, rows_ref in enumerate((keep_ref, came_ref)):
        for peer in range(rows_ref.shape[0] // share):
            out_ref[peer, side * share : (side + 1) * share, :] = rows_ref[peer * share : (peer + 1) * share, :]


def place_kernel(got_ref, target_ref, energy_ref):
    tok, width = target_ref.shape
    meta = got_ref[:, width:].astype(F32).T
    slot = (meta[0:1] * 16.0 + meta[1:2]).astype(jnp.int32)
    here = iota((tok, tok), 0) == slot
    pick = jnp.where(here, 1.0, 0.0).astype(BF16)

    def placed(row):
        return jnp.sum(jnp.where(here, row, 0.0), axis=1, keepdims=True)

    rows = jnp.dot(pick, got_ref[:, :width], preferred_element_type=F32)
    target_ref[...] = (rows * placed(scale_of(meta[2:3]))).astype(BF16)
    squares = placed(meta[3:4] + meta[4:5] + meta[5:6])
    energy_ref[...] = jnp.broadcast_to(squares / TW + 1e-05, (tok, META))


def project_kernel(own_ref, sib_ref, adapter_ref, out_ref):
    rows = jnp.concatenate([own_ref[...], sib_ref[...]], axis=0)
    out_ref[...] = jnp.dot(rows, adapter_ref[...], preferred_element_type=F32)


def project_call(own, sib, adapter):
    half, depth = own.shape
    width = adapter.shape[1]
    tile = 384
    return pl.pallas_call(
        project_kernel,
        out_shape=jax.ShapeDtypeStruct((2 * half, width), F32),
        grid=(width // tile,),
        in_specs=[
            pl.BlockSpec((half, depth), lambda n: (0, 0)),
            pl.BlockSpec((half, depth), lambda n: (0, 0)),
            pl.BlockSpec((depth, tile), lambda n: (0, n)),
        ],
        out_specs=pl.BlockSpec((2 * half, tile), lambda n: (0, n)),
        compiler_params=params(14),
        cost_estimate=LIGHT,
        name="project",
    )(own, sib, adapter)


def delta_kernel(where_ref, p0_ref, p1_ref, p2_ref, p3_ref, target_ref, energy_ref, delta_ref):
    half = p0_ref.shape[0] // 2
    zh, core = where_ref[3], where_ref[4]
    step = 1 - 2 * core
    for s, p_ref in enumerate((p0_ref, p1_ref, p2_ref, p3_ref)):
        mine = ((zh - step * s + 4) % 4) * 2 + core
        sibs = ((zh + step * s + 4) % 4) * 2 + 1 - core
        for side, block in enumerate((mine, sibs)):
            token = pl.ds(pl.multiple_of(block * half, half), half)
            diff = p_ref[side * half : (side + 1) * half, :] - target_ref[token, :].astype(F32)
            at = (2 * s + side) * half
            delta_ref[at : at + half, :] = (diff / energy_ref[token, :1]).astype(BF16)


def row_kernel(delta_ref, adapter_ref, *refs):
    keeps, send_ref = refs[:4], refs[4]
    half = keeps[0].shape[0]
    term = lax.dot_general(delta_ref[...], adapter_ref[...], (((1,), (1,)), ((), ())), preferred_element_type=F32)
    for s in range(4):
        keeps[s][...] = term[2 * s * half : (2 * s + 1) * half]
        send_ref[s * half : (s + 1) * half, :] = term[(2 * s + 1) * half : (2 * s + 2) * half].astype(BF16)


def row_call(delta, adapter):
    tok, width = delta.shape
    half = tok // 8
    depth = adapter.shape[0]
    tile = 512
    return pl.pallas_call(
        row_kernel,
        out_shape=(jax.ShapeDtypeStruct((half, depth), F32),) * 4 + (jax.ShapeDtypeStruct((4 * half, depth), BF16),),
        grid=(depth // tile,),
        in_specs=[
            pl.BlockSpec((tok, width), lambda n: (0, 0)),
            pl.BlockSpec((tile, width), lambda n: (n, 0)),
        ],
        out_specs=(pl.BlockSpec((half, tile), lambda n: (0, n)),) * 4
        + (pl.BlockSpec((4 * half, tile), lambda n: (0, n)),),
        compiler_params=params(11),
        cost_estimate=LIGHT,
        name="row_terms",
    )(delta, adapter)


def weight_kernel(k, side, with_came, where_ref, *refs):
    hidden, delta = refs[:8], refs[8]
    came = refs[9:11] if with_came else (None, None)
    outs, left = refs[9 + 2 * with_came : -1], refs[-1]
    half = hidden[0].shape[0]
    x, y, core = where_ref[1], where_ref[2], where_ref[4]
    ahead = k * (1 - 2 * core) + 4
    for chunk in range(2):
        for at in range(2):
            j = 2 * side + at
            if chunk == 0:
                block = ((x + ahead) % 4) * 4 + (y + j) % 4
            else:
                block = 16 + ((x + j) % 4) * 4 + (y + ahead) % 4
            columns = pl.ds(pl.multiple_of(block * 128, 128), 128)
            for part in range(8):
                left[part * half : (part + 1) * half, at * 128 : (at + 1) * 128] = hidden[part][:, columns]
        term = lax.dot_general(left[...], delta[...], (((0,), (0,)), ((), ())), preferred_element_type=F32)
        if with_came:
            term = term + came[chunk][...].astype(F32)
        if k == 0:
            for at in range(2):
                out = outs[2 * chunk + at]
                out[...] = term[128 * at : 128 * (at + 1)].astype(out.dtype)
        else:
            outs[chunk][...] = term.astype(BF16)


def weight_call(k, side, where, hidden, delta, came=()):
    tokens = 8 * hidden[0].shape[0]
    width = delta.shape[1]
    vmem = pl.BlockSpec(memory_space=pltpu.VMEM)
    if k == 0:
        kinds = [jax.ShapeDtypeStruct((128, width), BF16 if side else F32), jax.ShapeDtypeStruct((128, width), BF16)]
    else:
        kinds = [jax.ShapeDtypeStruct((256, width), BF16)]
    return pl.pallas_call(
        functools.partial(weight_kernel, k, side, len(came) > 0),
        out_shape=tuple(kinds * 2),
        in_specs=[pl.BlockSpec(memory_space=pltpu.SMEM)] + [vmem] * (9 + len(came)),
        out_specs=(vmem,) * (2 * len(kinds)),
        scratch_shapes=[pltpu.VMEM((tokens, 256), BF16)],
        compiler_params=params(18),
        cost_estimate=LIGHT,
        name=f"weight_{k}_{side}",
    )(where, *hidden, delta, *came)


def light(kernel, name, out_shape, mib, *args, scalars=0):
    vmem = pl.BlockSpec(memory_space=pltpu.VMEM)
    return pl.pallas_call(
        kernel,
        out_shape=tuple(out_shape),
        in_specs=[pl.BlockSpec(memory_space=pltpu.SMEM)] * scalars + [vmem] * (len(args) - scalars),
        out_specs=(vmem,) * len(out_shape),
        compiler_params=params(mib),
        cost_estimate=LIGHT,
        name=name,
    )(*args)


def shard_kernel(where, own_a, a1, a2, a3, own_b, b1, b2, b3, stay, leave):
    sum_a = own_a[...] + a1[...].astype(F32) + a2[...].astype(F32) + a3[...].astype(F32)
    sum_b = own_b[...] + b1[...].astype(F32) + b2[...].astype(F32) + b3[...].astype(F32)
    low = where[0] == 0
    stay[...] = jnp.where(low, sum_a, sum_b)
    leave[...] = jnp.where(low, sum_b, sum_a).astype(BF16)


def weight_out_kernel(tokens, stay, came, out):
    out[...] = ((stay[...] + came[...].astype(F32)) / tokens).astype(BF16)


def row_out_kernel(pair, came, out):
    out[...] = (pair[...] + came[...].astype(F32)).astype(BF16)


def pair_kernel(k0, k1, k2, k3, swapped, *outs):
    half = k0.shape[0]
    for s, keep in enumerate((k0, k1, k2, k3)):
        total = keep[...] + swapped[s * half : (s + 1) * half, :].astype(F32)
        outs[s][...] = total.astype(outs[s].dtype)


def on_device(hidden, adapter, teacher_rows, scale_exps, packing):
    tok, width = teacher_rows.shape
    half = hidden.shape[0]
    peers = lax.axis_size("dp")
    dp, tensor = lax.axis_index("dp"), lax.axis_index("tensor")
    zl, x, y = dp // 16, (dp // 4) % 4, dp % 4
    zh, core = tensor // 2, tensor % 2

    def over_dp(move):
        pairs = []
        for i in range(32):
            a, b, c = move(i // 16, (i // 4) % 4, i % 4)
            pairs.append((i, (a % 2) * 16 + (b % 4) * 4 + c % 4))
        return lambda value: lax.ppermute(value, "dp", pairs)

    def over_tensor(move):
        pairs = []
        for i in range(8):
            a, b = move(i // 2, i % 2)
            pairs.append((i, (a % 4) * 2 + b % 2))
        return lambda value: lax.ppermute(value, "tensor", pairs)

    def by_core(move):
        pairs = []
        for i in range(256):
            d, t = i // 8, i % 8
            b, c = move((d // 4) % 4, d % 4, 1 - 2 * (t % 2))
            pairs.append((i, ((d // 16) * 16 + (b % 4) * 4 + c % 4) * 8 + t))
        return lambda value: lax.ppermute(value, ("dp", "tensor"), pairs)

    x_ring = by_core(lambda b, c, way: (b + way, c))
    y_ring = by_core(lambda b, c, way: (b, c + way))
    x_forth, x_back = over_dp(lambda a, b, c: (a, b + 1, c)), over_dp(lambda a, b, c: (a, b - 1, c))
    y_forth, y_back = over_dp(lambda a, b, c: (a, b, c + 1)), over_dp(lambda a, b, c: (a, b, c - 1))
    x_across, y_across = over_dp(lambda a, b, c: (a, b + 2, c)), over_dp(lambda a, b, c: (a, b, c + 2))
    z_swap = over_dp(lambda a, b, c: (a + 1, b, c))
    core_swap = over_tensor(lambda a, b: (a, b + 1))
    chain = over_tensor(lambda a, b: (a + 1 - 2 * b, b))

    where = jnp.stack([zl, x, y, zh, core]).astype(jnp.int32)
    row = jax.ShapeDtypeStruct((1, tok), F32)
    share = tok // peers
    lanes = width + META
    packing, scale_exps = packing.reshape(1, tok), scale_exps.reshape(1, tok)

    squares = light(squares_kernel, "squares", (row,), 10, scale_exps, teacher_rows)[0]
    squares = light(sum_kernel, "pair_squares", (row,), 4, squares, core_swap(squares))[0]
    others = [over_tensor(lambda a, b, k=k: (a + k, b))(squares) for k in (1, 2, 3)]
    own = [hidden, chain(hidden)]
    own[1], *others = lax.optimization_barrier((own[1], *others))
    half_rows = jax.ShapeDtypeStruct((tok // 2, lanes), BF16)
    keep, leave = light(
        functools.partial(pack_kernel, share), "pack", (half_rows, half_rows), 18,
        where, packing, scale_exps, squares, *others, teacher_rows, scalars=1,
    )
    came = z_swap(leave)
    own.append(chain(own[1]))
    sib = [core_swap(block) for block in own]
    projected = [project_call(own[s], sib[s], adapter) for s in range(3)]
    came, *projected[:2] = lax.optimization_barrier((came, *projected[:2]))
    own.append(chain(own[2]))
    own[3], projected[2] = lax.optimization_barrier((own[3], projected[2]))
    sib.append(core_swap(own[3]))
    merged = light(
        functools.partial(merge_kernel, share), "merge",
        (jax.ShapeDtypeStruct((peers // 2, 2 * share, lanes), BF16),), 10, keep, came,
    )[0]
    groups = [list(range(peers // 2)), list(range(peers // 2, peers))]
    got = lax.all_to_all(merged, "dp", 0, 0, axis_index_groups=groups, tiled=True)
    got, projected[2] = lax.optimization_barrier((got, projected[2]))
    target, energy = light(
        place_kernel, "place",
        (jax.ShapeDtypeStruct((tok, width), BF16), jax.ShapeDtypeStruct((tok, META), F32)), 16,
        got.reshape(tok, lanes),
    )
    last, target = lax.optimization_barrier((sib[3], target))
    projected.append(project_call(own[3], last, adapter))
    delta = light(
        delta_kernel, "delta", (jax.ShapeDtypeStruct((tok, width), BF16),), 12,
        where, *projected, target, energy, scalars=1,
    )[0]

    held = [part for pair in zip(own, sib) for part in pair]
    def step(k, side, given, came=()):
        ring_a, ring_b = weight_call(k, side, where, held, given, came)
        return ring_a, (x_ring(ring_a), y_ring(ring_b))

    mark, came_0 = step(3, 0, delta)
    later, _ = lax.optimization_barrier((delta, mark))
    mark, came_1 = step(3, 1, later)
    later, _ = lax.optimization_barrier((delta, mark))
    *keeps, send = row_call(later, adapter)
    *came_0, send = lax.optimization_barrier((*came_0, send))
    mark, came_0 = step(2, 0, delta, came_0)
    *came_1, _ = lax.optimization_barrier((*came_1, mark))
    mark, came_1 = step(2, 1, delta, came_1)
    send, _ = lax.optimization_barrier((send, mark))
    swapped = core_swap(send)
    block = jax.ShapeDtypeStruct((half, hidden.shape[1]), F32)
    block16 = jax.ShapeDtypeStruct(block.shape, BF16)
    pair = light(pair_kernel, "pair", (block, block16, block, block), 14, *keeps, swapped)
    total = chain(pair[1])
    *came_0, _ = lax.optimization_barrier((*came_0, pair[1]))
    mark, came_0 = step(1, 0, delta, came_0)
    *came_1, _ = lax.optimization_barrier((*came_1, mark))
    mark, came_1 = step(1, 1, delta, came_1)
    total, _ = lax.optimization_barrier((total, mark))
    sent = light(row_out_kernel, "row_2", (block16,), 8, pair[2], total)[0]
    total = chain(sent)
    *came_0, _ = lax.optimization_barrier((*came_0, sent))
    own_a, a1, own_b, b1 = weight_call(0, 0, where, held, delta, came_0)
    came = [y_forth(a1), x_forth(b1)]
    *came_1, _ = lax.optimization_barrier((*came_1, a1))
    a2, a3, b2, b3 = weight_call(0, 1, where, held, delta, came_1)
    *came, total, _ = lax.optimization_barrier((*came, total, a2))
    total = chain(light(row_out_kernel, "row_3", (block16,), 8, pair[3], total)[0])
    came = (came[0], y_across(a2), y_back(a3), came[1], x_across(b2), x_back(b3))
    *came, total = lax.optimization_barrier((*came, total))
    part = jax.ShapeDtypeStruct((128, width), F32)
    part16 = jax.ShapeDtypeStruct((128, width), BF16)
    stay, leave = light(
        shard_kernel, "shard", (part, part16), 10, where, own_a, *came[:3], own_b, *came[3:], scalars=1,
    )
    weight_grad = light(
        functools.partial(weight_out_kernel, tok), "weight_out", (part16,), 8, stay, z_swap(leave)
    )[0]
    row_grad = light(row_out_kernel, "row_0", (block16,), 8, pair[0], total)[0]
    return row_grad, weight_grad


def solution(mesh):
    placed = (P(("dp", "tensor"), None), P(None, "tensor"), P("dp", "tensor"), P("dp"), P("dp"))
    return jax.shard_map(
        on_device,
        mesh=mesh,
        in_specs=placed,
        out_specs=(P(("dp", "tensor"), None), P("dp", "tensor")),
        check_vma=False,
    )
```
